32 devices in a mesh: section: 4 (over z), tp: 4 (over y, core), mirror: 2 (over x).
Axes of the slice: x: 2, y: 2, z: 4, core: 2. Of those that a mesh axis runs over, the one named last changes fastest.
Arguments:
- hidden: bfloat16 [2, 4, 2, 128, 14336], P(None, 'section', 'mirror', None, 'tp'), may hold values from -6 to 6
- incoming: bfloat16 [2, 4, 2, 128, 4096], P(None, 'section', 'mirror', None, 'tp'), may hold values from -0.3984375 to 0.3984375
- block_mask: int32 [2, 112, 32], P(None, 'tp'), may hold values from 0 to 1, as said below
Outputs:
- block_grads: bfloat16 [4, 4, 252, 128, 128], P('section', 'tp', 'mirror')
The draws below stay inside these ranges and needn't reach their ends.
Inputs may be any that keep to these rules, and one draw needn't show every extreme that they name: `block_mask`: for every section and every index of tp, its 28 block rows keep between 7/16 and 9/16 of their blocks, at most 504; in every section exactly 504 on some index of tp.
All inputs are finite; a program needn't handle non-finite values.
Results may differ from the reference program's by a relative error of at most 0.006.
Values may be sent and summed in bfloat16 or wider, within the bound.
A program may use at most 128 MiB of HBM per device.

```python
import jax
import jax.numpy as jnp
from jax import lax

D = 4096
FF = 14336
BLK = 128
ROWS = 128
NSTG = 2
FFB = 28
DB = 32
KCAP = 504
N_SECTION = 4
N_TP = 4
N_MIRROR = 2


def draw_block_mask(key, part):
    blocks = FFB * DB
    key_counts = jax.random.fold_in(key, 11)
    key_busiest = jax.random.fold_in(key, 12)
    key_scores = jax.random.fold_in(key, 13)
    counts_base = jax.random.randint(key_counts, (NSTG, N_TP), blocks * 7 // 16, KCAP + 1)
    busiest = jax.random.randint(key_busiest, (NSTG,), 0, N_TP)
    counts = jnp.where(jnp.arange(N_TP)[None, :] == busiest[:, None], KCAP, counts_base)
    scores = jax.random.randint(key_scores, (NSTG, N_TP, blocks), 0, 1 << 20) * blocks + jnp.arange(blocks)[None, None, :]
    ordering = jnp.argsort(scores, axis=-1, stable=True)
    rank_table = jnp.argsort(ordering, axis=-1, stable=True)
    kept_flags = (rank_table < counts[:, :, None]).astype(jnp.int32)
    return kept_flags.reshape(NSTG, N_TP * FFB, DB)


def level_of(key, extent, cuts, low, top_value):
    factor_of = 1.0
    for dim, parts in cuts:
        draws = jax.random.uniform(jax.random.fold_in(jax.random.fold_in(key, 6), dim), (parts,), jnp.float32, low / len(cuts), top_value / len(cuts))
        factor_of = factor_of * jnp.repeat(jnp.exp(draws), extent[dim] // parts).reshape((-1,) + (1,) * (len(extent) - 1 - dim))
    return factor_of


def gaussian(rng, shape, width, limit, shards=(), kind=jnp.bfloat16):
    loudness = level_of(rng, shape, shards, -0.22, 0.18) if shards else 1.0
    array = jax.random.normal(rng, shape, jnp.float32) * width * loudness
    return jnp.minimum(jnp.maximum(array, -limit), limit).astype(kind)


def setup_inputs(seed: int = 0) -> dict:
    seeds = jax.random.split(jax.random.key(seed), 4)
    hidden = gaussian(seeds[0], (2, N_SECTION, N_MIRROR, ROWS, FF), 1.0, 6.0, ((1, 4), (2, 2), (4, 4)))
    incoming = gaussian(seeds[1], (2, N_SECTION, N_MIRROR, ROWS, D), 0.05, 0.3984375, ((1, 4), (2, 2), (4, 4)))
    block_mask = draw_block_mask(jax.random.fold_in(seeds[3], 71), 0)
    return dict(hidden=hidden, incoming=incoming, block_mask=block_mask)


def slot_table(mask_local, slot_total):
    flat = mask_local.reshape(-1).astype(jnp.int32)
    running = jnp.cumsum(flat).astype(jnp.int32)
    positions = jnp.arange(slot_total, dtype=jnp.int32)
    targets = jnp.sum((running[None, :] <= positions[:, None]).astype(jnp.int32), axis=1).astype(jnp.int32)
    usable = positions < running[-1]
    targets = jnp.minimum(targets, flat.shape[0] - 1).astype(jnp.int32)
    columns_count = mask_local.shape[1]
    return (targets // columns_count).astype(jnp.int32), (targets % columns_count).astype(jnp.int32), usable


def block_partials(hidden_rows, cotangent, block_rows, block_cols, usable):
    row_total = hidden_rows.shape[0]
    hidden_blocks = hidden_rows.astype(jnp.float32).reshape(row_total, -1, BLK)
    cot_blocks = cotangent.astype(jnp.float32).reshape(row_total, -1, BLK)
    left = jnp.take(hidden_blocks, block_rows, axis=1)
    right = jnp.take(cot_blocks, block_cols, axis=1)
    product = jnp.einsum('nkc,nkd->kcd', left, right)
    product = jnp.where(usable[:, None, None], product, jnp.zeros_like(product))
    return product.astype(jnp.bfloat16)


def reference(hidden, incoming, block_mask):
    arrived_down = jnp.roll(incoming[0], -1, axis=0)
    arrived_up = jnp.roll(incoming[1], 1, axis=0)
    arrived = jnp.stack([arrived_down, arrived_up])
    ff_shard = FF // N_TP

    def section_shard(index):
        section_id = (index // N_TP).astype(jnp.int32)
        shard = (index % N_TP).astype(jnp.int32)
        mask_local = lax.dynamic_slice(block_mask, (section_id, shard * FFB, jnp.int32(0)), (1, FFB, DB))[0]
        block_rows, block_cols, usable = slot_table(mask_local, KCAP)
        replica_sums = []
        for mirror_id in range(N_MIRROR):
            replica_terms = []
            for half_index in range(2):
                position = section_id + half_index * NSTG
                hidden_rows = lax.dynamic_slice(hidden, (jnp.int32(0), position, jnp.int32(mirror_id), jnp.int32(0), shard * ff_shard), (2, 1, 1, ROWS, ff_shard)).reshape(2 * ROWS, ff_shard)
                cotangent = lax.dynamic_slice(arrived, (jnp.int32(0), position, jnp.int32(mirror_id), jnp.int32(0), jnp.int32(0)), (2, 1, 1, ROWS, D)).reshape(2 * ROWS, D)
                replica_terms.append(block_partials(hidden_rows, cotangent, block_rows, block_cols, usable))
            paired = (replica_terms[0].astype(jnp.float32) + replica_terms[1].astype(jnp.float32)).astype(jnp.bfloat16)
            replica_sums.append(paired)
        return (replica_sums[0].astype(jnp.float32) + replica_sums[1].astype(jnp.float32)).astype(jnp.bfloat16)

    grads = lax.map(section_shard, jnp.arange(NSTG * N_TP, dtype=jnp.int32))
    grads = grads.reshape(NSTG, N_TP, 2, KCAP // 2, BLK, BLK)
    grads = jnp.transpose(grads, (2, 0, 1, 3, 4, 5)).reshape(N_SECTION, N_TP, KCAP // 2, BLK, BLK)
    return grads
```

```python
import functools

import jax
import jax.numpy as jnp
from jax import lax
from jax.experimental import pallas as pl
from jax.experimental.pallas import tpu as pltpu
from jax.sharding import PartitionSpec as P

BLK = 128
MESH = pl.DeviceIdType.MESH


def cdiv(a, b):
    return -(-a // b)


def windows(rows, cols):
    kept_min, cap = rows * cols * 7 // 16, rows * cols * 9 // 16

    def span(first, last):
        return first // cols, min(rows - 1, rows - max(1, cdiv(kept_min - last, cols)))

    halves = [span(h * cap // 2, (h + 1) * cap // 2 - 1) for h in range(2)]
    quarters = [span(q * cap // 4, (q + 1) * cap // 4 - 1) for q in range(4)]
    hw = max(b - a + 1 for a, b in halves)
    qw = max(b - a + 1 for a, b in quarters)
    hs = [min(a, rows - hw) for a, _ in halves]
    qs = [min(a, rows - qw) for a, _ in quarters]
    for q in range(4):
        h = q // 2
        qs[q] = max(hs[h], min(qs[q], hs[h] + hw - qw))
        assert qs[q] <= quarters[q][0] and qs[q] + qw > quarters[q][1]
        assert hs[h] <= halves[h][0] and hs[h] + hw > halves[h][1]
    return hw, qw, hs, qs


def pick(table, half, m):
    return (1 - half) * ((1 - m) * table[0] + m * table[1]) + half * ((1 - m) * table[2] + m * table[3])


def flip(u, bit):
    return u + bit * (1 - 2 * ((u // bit) % 2))


def flips(u, mask, top):
    bit = 1
    while bit < top:
        if mask & bit:
            u = flip(u, bit)
        bit *= 2
    return u


def kernel(sizes, rel_ref, col_ref, use_ref, h_ref, inc_ref, out_ref,
           inc_b, c00, c01, c10, c11, zh, xh0, xh1, h_t, acc,
           zc_s, zc_r, zh_s, zh_r, xo_s, xo_r, xr_s, xr_r, xc_s, xc_r, tc_s, tc_r):
    S, T, rows, hw, qw, hs, qs, slots, nch, unroll, cpt = sizes
    p, t, m = lax.axis_index("section"), lax.axis_index("tp"), lax.axis_index("mirror")
    half = p // (S // 2)
    other = 1 - m
    hstart = (1 - half) * hs[0] + half * hs[1]
    hstart_there = half * hs[0] + (1 - half) * hs[1]
    qstart = pick(qs, half, m)
    qstart_there = pick(qs, half, other)
    partner = (p + S // 2) % S
    C = ((c00, c01), (c10, c11))

    def cols(start, n):
        return pl.ds(pl.multiple_of(start * BLK, BLK), n * BLK)

    mine = pl.ds(t * cpt, cpt)

    offsets = sorted({(sgn + s * (S // 2)) % S for sgn in (1, -1) for s in (0, 1)} | {S // 2})
    bits = []
    b = T // 2
    while b >= 1:
        bits.append(b)
        b //= 2
    peers = [{"section": (p + o) % S} for o in offsets] + [{"mirror": other}] + [{"tp": flip(t, b)} for b in bits]
    barrier = pltpu.get_barrier_semaphore()
    for peer in peers:
        pl.semaphore_signal(barrier, inc=1, device_id=peer, device_id_type=MESH)
    for d in range(2):
        for c in range(cpt):
            inc_b[d, c] = inc_ref[d, :, c * BLK:(c + 1) * BLK]
    pl.semaphore_wait(barrier, len(peers))

    def copy(src, dst, ss, rs, dev):
        return pltpu.make_async_remote_copy(
            src_ref=src, dst_ref=dst, send_sem=ss, recv_sem=rs, device_id=dev, device_id_type=MESH)

    zc = {}
    for s in range(2):
        for d in range(2):
            i = 2 * s + d
            dest = (p + (S - 1 if d == 0 else 1) + s * (S // 2)) % S
            zc[s, d] = copy(inc_b.at[d], C[s][0].at[d, mine], zc_s.at[i], zc_r.at[i], {"section": dest})
    per = nch // 2
    step = rows // per
    zhc, xr = [], []
    for i in range(nch):
        d, r = i // per, pl.ds((i % per) * step, step)
        zhc.append(copy(h_ref.at[d, r, cols(hstart_there, hw)], zh.at[d, r], zh_s.at[i], zh_r.at[i],
                        {"section": partner}))
        xr.append(copy(zh.at[d, r, cols(qstart_there - hstart, qw)], xh1.at[d, r], xr_s.at[i], xr_r.at[i],
                       {"mirror": other}))
    xo = [copy(h_ref.at[d, :, cols(qstart_there, qw)], xh0.at[d], xo_s.at[d], xo_r.at[d], {"mirror": other})
          for d in range(2)]
    xc = {}
    for s in range(2):
        for d in range(2):
            i = 2 * s + d
            xc[s, d] = copy(C[s][0].at[d, mine], C[s][1].at[d, mine], xc_s.at[i], xc_r.at[i], {"mirror": other})
    tc = {}
    stage_rels = []
    have = [0]
    for k, b in enumerate(bits):
        stage_rels.append(list(have))
        have = have + [r | b for r in have]
    for s in range(2):
        for d in range(2):
            for mr in range(2):
                n = ((s * 2 + d) * 2 + mr) * (T - 1)
                for k, b in enumerate(bits):
                    for r in stage_rels[k]:
                        u = flips(t, r, T)
                        ref = C[s][mr].at[d, pl.ds(u * cpt, cpt)]
                        tc[s, d, mr, k, r] = copy(ref, ref, tc_s.at[n], tc_r.at[n], {"tp": flip(t, b)})
                        n += 1

    def spread(s, d, mr, r, after):
        for k in range(after + 1, len(bits)):
            tc[s, d, mr, k, r].start()

    def stage_wait(s, mr, k):
        for d in range(2):
            for r in stage_rels[k]:
                tc[s, d, mr, k, r].wait_recv()
                spread(s, d, mr, r | bits[k], k)

    def relay(i):
        zhc[i].wait_recv()
        xr[i].start()
        zhc[i].wait_send()
        if i + 2 < nch:
            zhc[i + 2].start()

    def compute(s, mr, src, first, kind):
        def turn(b, carry):
            blk = src[:, :, cols(first + b, 1)].reshape(2 * rows, BLK)
            h_t[b] = blk.T
            return carry

        lax.fori_loop(0, qw, turn, 0)
        cot = C[s][mr]

        def group(g, carry):
            for e in range(unroll):
                k = g * unroll + e
                right = cot[:, col_ref[k]].reshape(2 * rows, BLK)
                got = jnp.dot(h_t[rel_ref[k]], right, preferred_element_type=jnp.float32)
                if kind != "first":
                    got = got + acc[k]
                if kind == "last":
                    out_ref[k] = (got * use_ref[k]).astype(out_ref.dtype)
                else:
                    acc[k] = got
            return carry

        lax.fori_loop(0, slots // unroll, group, 0)

    for d in range(2):
        for s in range(2):
            zc[s, d].start()
    for c in xo:
        c.start()
    zhc[0].start()
    zhc[1].start()
    for s in range(2):
        for d in range(2):
            zc[s, d].wait_recv()
            xc[s, d].start()
            spread(s, d, 0, 0, -1)
    for s in range(2):
        for d in range(2):
            xc[s, d].wait_recv()
            spread(s, d, 1, 0, -1)
    relay(0)
    relay(1)
    for k in range(len(bits)):
        stage_wait(0, 0, k)
    compute(0, 0, h_ref, qstart, "first")
    relay(2)
    for k in range(len(bits)):
        stage_wait(0, 1, k)
    for c in xo:
        c.wait_recv()
    relay(3)
    compute(0, 1, xh0, 0, "add")
    for i in range(4, nch):
        relay(i)
    for mr in range(2):
        for k in range(len(bits)):
            stage_wait(1, mr, k)
    compute(1, 0, zh, qstart - hstart, "add")
    for c in xr:
        c.wait_recv()
    compute(1, 1, xh1, 0, "last")
    for c in list(zc.values()) + xo + list(xc.values()) + list(tc.values()) + xr:
        c.wait_send()


def body(hidden, incoming, block_mask):
    S, T = lax.axis_size("section"), lax.axis_size("tp")
    p, m = lax.axis_index("section"), lax.axis_index("mirror")
    _, ffb, db = block_mask.shape
    rows, ff, dm = hidden.shape[3], hidden.shape[4], incoming.shape[4]
    cap = ffb * db * 9 // 16
    slots = cap // 4
    hw, qw, hs, qs = windows(ffb, db)
    half = p // (S // 2)
    mask = lax.dynamic_index_in_dim(block_mask, p % (S // 2), 0, keepdims=False)
    running = jnp.cumsum(mask.reshape(-1))
    positions = (2 * half + m) * slots + jnp.arange(slots, dtype=jnp.int32)
    targets = jnp.sum((running[None, :] <= positions[:, None]).astype(jnp.int32), axis=1)
    use = (positions < running[-1]).astype(jnp.float32)
    targets = jnp.minimum(targets, ffb * db - 1)
    rel = jnp.clip(targets // db - pick(qs, half, m), 0, qw - 1)
    col = targets % db
    per_t = dm // BLK
    nch = 8
    unroll = max(u for u in range(1, 10) if slots % u == 0)
    sizes = (S, T, rows, hw, qw, hs, qs, slots, nch, unroll, per_t)
    bf = jnp.bfloat16
    vmem, smem = pl.BlockSpec(memory_space=pltpu.VMEM), pl.BlockSpec(memory_space=pltpu.SMEM)
    dma = pltpu.SemaphoreType.DMA
    n_tc = 8 * (T - 1)
    out = pl.pallas_call(
        functools.partial(kernel, sizes),
        out_shape=jax.ShapeDtypeStruct((slots, BLK, BLK), bf),
        in_specs=[smem] * 3 + [vmem] * 2,
        out_specs=vmem,
        scratch_shapes=[pltpu.VMEM((2, per_t, rows, BLK), bf)] + [pltpu.VMEM((2, db, rows, BLK), bf)] * 4
        + [pltpu.VMEM((2, rows, hw * BLK), bf)]
        + [pltpu.VMEM((2, rows, qw * BLK), bf)] * 2
        + [pltpu.VMEM((qw, BLK, 2 * rows), bf), pltpu.VMEM((slots, BLK, BLK), jnp.float32)]
        + [dma((4,)), dma((4,)), dma((nch,)), dma((nch,)), dma((2,)), dma((2,)), dma((nch,)), dma((nch,)),
           dma((4,)), dma((4,)), dma((n_tc,)), dma((n_tc,))],
        compiler_params=pltpu.CompilerParams(
            collective_id=0, has_side_effects=True, vmem_limit_bytes=48 * 1024 * 1024),
        cost_estimate=pl.CostEstimate(
            flops=slots * BLK * BLK * rows * 16, bytes_accessed=8 * 1024 * 1024, transcendentals=0),
    )(rel.astype(jnp.int32), col.astype(jnp.int32), use,
      hidden.reshape(2, rows, ff), incoming.reshape(2, rows, dm))
    return out.reshape(1, 1, slots, BLK, BLK)


def solution(mesh):
    placed = (
        P(None, "section", "mirror", None, "tp"),
        P(None, "section", "mirror", None, "tp"),
        P(None, "tp", None),
    )
    return jax.shard_map(
        body,
        mesh=mesh,
        in_specs=placed,
        out_specs=P("section", "tp", "mirror", None, None),
        check_vma=False,
    )
```

```python
import functools

import jax
import jax.numpy as jnp
from jax import lax
from jax.experimental import pallas as pl
from jax.experimental.pallas import tpu as pltpu
from jax.sharding import PartitionSpec as P

BLK = 128
MESH = pl.DeviceIdType.MESH


def cdiv(a, b):
    return -(-a // b)


def windows(rows, cols):
    kept_min, cap = rows * cols * 7 // 16, rows * cols * 9 // 16

    def span(first, last):
        return first // cols, min(rows - 1, rows - max(1, cdiv(kept_min - last, cols)))

    halves = [span(h * cap // 2, (h + 1) * cap // 2 - 1) for h in range(2)]
    quarters = [span(q * cap // 4, (q + 1) * cap // 4 - 1) for q in range(4)]
    hw = max(b - a + 1 for a, b in halves)
    qw = max(b - a + 1 for a, b in quarters)
    hs = [min(a, rows - hw) for a, _ in halves]
    qs = [min(a, rows - qw) for a, _ in quarters]
    for q in range(4):
        h = q // 2
        qs[q] = max(hs[h], min(qs[q], hs[h] + hw - qw))
        assert qs[q] <= quarters[q][0] and qs[q] + qw > quarters[q][1]
        assert hs[h] <= halves[h][0] and hs[h] + hw > halves[h][1]
    return hw, qw, hs, qs


def pick(table, half, m):
    return (1 - half) * ((1 - m) * table[0] + m * table[1]) + half * ((1 - m) * table[2] + m * table[3])


def flip(u, bit):
    return u + bit * (1 - 2 * ((u // bit) % 2))


def flips(u, mask, top):
    bit = 1
    while bit < top:
        if mask & bit:
            u = flip(u, bit)
        bit *= 2
    return u


def kernel(sizes, rel_ref, col_ref, use_ref, h_ref, inc_ref, out_ref,
           inc_b, c00, c01, c10, c11, zh, xh0, xh1, h_t, acc, inc_v, own, in_s,
           zc_s, zc_r, zh_s, zh_r, xo_s, xo_r, xr_s, xr_r, xc_s, xc_r, tc_s, tc_r):
    S, T, rows, hw, qw, hs, qs, slots, nch, unroll, cpt = sizes
    p, t, m = lax.axis_index("section"), lax.axis_index("tp"), lax.axis_index("mirror")
    half = p // (S // 2)
    other = 1 - m
    hstart = (1 - half) * hs[0] + half * hs[1]
    hstart_there = half * hs[0] + (1 - half) * hs[1]
    qstart = pick(qs, half, m)
    qstart_there = pick(qs, half, other)
    partner = (p + S // 2) % S
    C = ((c00, c01), (c10, c11))

    def cols(start, n):
        return pl.ds(pl.multiple_of(start * BLK, BLK), n * BLK)

    mine = pl.ds(t * cpt, cpt)

    offsets = sorted({(sgn + s * (S // 2)) % S for sgn in (1, -1) for s in (0, 1)} | {S // 2})
    bits = []
    b = T // 2
    while b >= 1:
        bits.append(b)
        b //= 2
    peers = [{"section": (p + o) % S} for o in offsets] + [{"mirror": other}] + [{"tp": flip(t, b)} for b in bits]
    barrier = pltpu.get_barrier_semaphore()
    for peer in peers:
        pl.semaphore_signal(barrier, inc=1, device_id=peer, device_id_type=MESH)
    fetch_inc = pltpu.make_async_copy(inc_ref, inc_v, in_s.at[0])
    fetch_own = pltpu.make_async_copy(h_ref.at[:, :, cols(qstart, qw)], own, in_s.at[1])
    fetch_inc.start()
    fetch_own.start()
    fetch_inc.wait()
    for d in range(2):
        for c in range(cpt):
            inc_b[d, c] = inc_v[d, :, c * BLK:(c + 1) * BLK]
    pl.semaphore_wait(barrier, len(peers))

    def copy(src, dst, ss, rs, dev):
        return pltpu.make_async_remote_copy(
            src_ref=src, dst_ref=dst, send_sem=ss, recv_sem=rs, device_id=dev, device_id_type=MESH)

    zc = {}
    for s in range(2):
        for d in range(2):
            i = 2 * s + d
            dest = (p + (S - 1 if d == 0 else 1) + s * (S // 2)) % S
            zc[s, d] = copy(inc_b.at[d], C[s][0].at[d, mine], zc_s.at[i], zc_r.at[i], {"section": dest})
    per = nch // 2
    step = rows // per
    zhc, xr = [], []
    for i in range(nch):
        d, r = i // per, pl.ds((i % per) * step, step)
        zhc.append(copy(h_ref.at[d, r, cols(hstart_there, hw)], zh.at[d, r], zh_s.at[i], zh_r.at[i],
                        {"section": partner}))
        xr.append(copy(zh.at[d, r, cols(qstart_there - hstart, qw)], xh1.at[d, r], xr_s.at[i], xr_r.at[i],
                       {"mirror": other}))
    xo = [copy(h_ref.at[d, :, cols(qstart_there, qw)], xh0.at[d], xo_s.at[d], xo_r.at[d], {"mirror": other})
          for d in range(2)]
    xc = {}
    for s in range(2):
        for d in range(2):
            i = 2 * s + d
            xc[s, d] = copy(C[s][0].at[d, mine], C[s][1].at[d, mine], xc_s.at[i], xc_r.at[i], {"mirror": other})
    tc = {}
    stage_rels = []
    have = [0]
    for k, b in enumerate(bits):
        stage_rels.append(list(have))
        have = have + [r | b for r in have]
    for s in range(2):
        for d in range(2):
            for mr in range(2):
                n = ((s * 2 + d) * 2 + mr) * (T - 1)
                for k, b in enumerate(bits):
                    for r in stage_rels[k]:
                        u = flips(t, r, T)
                        ref = C[s][mr].at[d, pl.ds(u * cpt, cpt)]
                        tc[s, d, mr, k, r] = copy(ref, ref, tc_s.at[n], tc_r.at[n], {"tp": flip(t, b)})
                        n += 1

    def spread(s, d, mr, r, after):
        for k in range(after + 1, len(bits)):
            tc[s, d, mr, k, r].start()

    def stage_wait(s, mr, k):
        for d in range(2):
            for r in stage_rels[k]:
                tc[s, d, mr, k, r].wait_recv()
                spread(s, d, mr, r | bits[k], k)

    ahead = 4

    def relay(i):
        zhc[i].wait_recv()
        xr[i].start()
        zhc[i].wait_send()
        if i + ahead < nch:
            zhc[i + ahead].start()

    def compute(lefts, rights, kind):
        def turn(b, carry):
            blk = jnp.concatenate([ref[d, :, cols(first + b, 1)] for ref, d, first in lefts], axis=0)
            h_t[b] = blk.T
            return carry

        lax.fori_loop(0, qw, turn, 0)

        def group(g, carry):
            for e in range(unroll):
                k = g * unroll + e
                right = jnp.concatenate([ref[d, col_ref[k]] for ref, d in rights], axis=0)
                got = jnp.dot(h_t[rel_ref[k]], right, preferred_element_type=jnp.float32)
                if kind != "first":
                    got = got + acc[k]
                if kind == "last":
                    out_ref[k] = (got * use_ref[k]).astype(out_ref.dtype)
                else:
                    acc[k] = got
            return carry

        lax.fori_loop(0, slots // unroll, group, 0)

    for d in range(2):
        for s in range(2):
            zc[s, d].start()
    for c in xo:
        c.start()
    zhc[0].start()
    zhc[1].start()
    for s in range(2):
        for d in range(2):
            zc[s, d].wait_recv()
            xc[s, d].start()
            spread(s, d, 0, 0, -1)
    zhc[2].start()
    zhc[3].start()
    for s in range(2):
        for d in range(2):
            xc[s, d].wait_recv()
            spread(s, d, 1, 0, -1)
    relay(0)
    relay(1)
    relay(2)
    for k in range(len(bits) - 1):
        for mr in range(2):
            stage_wait(0, mr, k)
    relay(3)
    last = len(bits) - 1
    stage_wait(0, 0, last)
    fetch_own.wait()
    compute([(own, 0, 0), (own, 1, 0)], [(c00, 0), (c00, 1)], "first")
    relay(4)
    stage_wait(0, 1, last)
    for c in xo:
        c.wait_recv()
    compute([(xh0, 0, 0), (xh0, 1, 0)], [(c01, 0), (c01, 1)], "add")
    relay(5)
    for k in range(len(bits)):
        for mr in range(2):
            stage_wait(1, mr, k)
    for c in xr[:per]:
        c.wait_recv()
    mid = qstart - hstart
    compute([(zh, 0, mid), (xh1, 0, 0)], [(c10, 0), (c11, 0)], "add")
    relay(6)
    relay(7)
    for c in xr[per:]:
        c.wait_recv()
    compute([(zh, 1, mid), (xh1, 1, 0)], [(c10, 1), (c11, 1)], "last")
    for c in list(zc.values()) + xo + list(xc.values()) + list(tc.values()) + xr:
        c.wait_send()


def body(hidden, incoming, block_mask):
    S, T = lax.axis_size("section"), lax.axis_size("tp")
    p, m = lax.axis_index("section"), lax.axis_index("mirror")
    _, ffb, db = block_mask.shape
    rows, ff, dm = hidden.shape[3], hidden.shape[4], incoming.shape[4]
    cap = ffb * db * 9 // 16
    slots = cap // 4
    hw, qw, hs, qs = windows(ffb, db)
    half = p // (S // 2)
    mask = lax.dynamic_index_in_dim(block_mask, p % (S // 2), 0, keepdims=False)
    running = jnp.cumsum(mask.reshape(-1))
    positions = (2 * half + m) * slots + jnp.arange(slots, dtype=jnp.int32)
    targets = jnp.sum((running[None, :] <= positions[:, None]).astype(jnp.int32), axis=1)
    use = (positions < running[-1]).astype(jnp.float32)
    targets = jnp.minimum(targets, ffb * db - 1)
    rel = jnp.clip(targets // db - pick(qs, half, m), 0, qw - 1)
    col = targets % db
    per_t = dm // BLK
    nch = 8
    unroll = max(u for u in range(1, 10) if slots % u == 0)
    sizes = (S, T, rows, hw, qw, hs, qs, slots, nch, unroll, per_t)
    bf = jnp.bfloat16
    vmem, smem = pl.BlockSpec(memory_space=pltpu.VMEM), pl.BlockSpec(memory_space=pltpu.SMEM)
    hbm = pl.BlockSpec(memory_space=pltpu.HBM)
    dma = pltpu.SemaphoreType.DMA
    n_tc = 8 * (T - 1)
    out = pl.pallas_call(
        functools.partial(kernel, sizes),
        out_shape=jax.ShapeDtypeStruct((slots, BLK, BLK), bf),
        in_specs=[smem] * 3 + [hbm] * 2,
        out_specs=vmem,
        scratch_shapes=[pltpu.VMEM((2, per_t, rows, BLK), bf)] + [pltpu.VMEM((2, db, rows, BLK), bf)] * 4
        + [pltpu.VMEM((2, rows, hw * BLK), bf)]
        + [pltpu.VMEM((2, rows, qw * BLK), bf)] * 2
        + [pltpu.VMEM((qw, BLK, 2 * rows), bf), pltpu.VMEM((slots, BLK, BLK), jnp.float32)]
        + [pltpu.VMEM((2, rows, dm), bf), pltpu.VMEM((2, rows, qw * BLK), bf), dma((2,))]
        + [dma((4,)), dma((4,)), dma((nch,)), dma((nch,)), dma((2,)), dma((2,)), dma((nch,)), dma((nch,)),
           dma((4,)), dma((4,)), dma((n_tc,)), dma((n_tc,))],
        compiler_params=pltpu.CompilerParams(
            collective_id=0, has_side_effects=True, vmem_limit_bytes=48 * 1024 * 1024),
        cost_estimate=pl.CostEstimate(
            flops=slots * BLK * BLK * rows * 16, bytes_accessed=8 * 1024 * 1024, transcendentals=0),
    )(rel.astype(jnp.int32), col.astype(jnp.int32), use,
      hidden.reshape(2, rows, ff), incoming.reshape(2, rows, dm))
    return out.reshape(1, 1, slots, BLK, BLK)


def solution(mesh):
    placed = (
        P(None, "section", "mirror", None, "tp"),
        P(None, "section", "mirror", None, "tp"),
        P(None, "tp", None),
    )
    return jax.shard_map(
        body,
        mesh=mesh,
        in_specs=placed,
        out_specs=P("section", "tp", "mirror", None, None),
        check_vma=False,
    )
```

```python
import functools

import jax
import jax.numpy as jnp
from jax import lax
from jax.experimental import pallas as pl
from jax.experimental.pallas import tpu as pltpu
from jax.sharding import PartitionSpec as P

BLK = 128
MESH = pl.DeviceIdType.MESH


def cdiv(a, b):
    return -(-a // b)


def windows(rows, cols):
    kept_min, cap = rows * cols * 7 // 16, rows * cols * 9 // 16

    def span(first, last):
        return first // cols, min(rows - 1, rows - max(1, cdiv(kept_min - last, cols)))

    halves = [span(h * cap // 2, (h + 1) * cap // 2 - 1) for h in range(2)]
    quarters = [span(q * cap // 4, (q + 1) * cap // 4 - 1) for q in range(4)]
    hw = max(b - a + 1 for a, b in halves)
    qw = max(b - a + 1 for a, b in quarters)
    hs = [min(a, rows - hw) for a, _ in halves]
    qs = [min(a, rows - qw) for a, _ in quarters]
    for q in range(4):
        h = q // 2
        qs[q] = max(hs[h], min(qs[q], hs[h] + hw - qw))
        assert qs[q] <= quarters[q][0] and qs[q] + qw > quarters[q][1]
        assert hs[h] <= halves[h][0] and hs[h] + hw > halves[h][1]
    return hw, qw, hs, qs


def pick(table, half, m):
    return (1 - half) * ((1 - m) * table[0] + m * table[1]) + half * ((1 - m) * table[2] + m * table[3])


def flip(u, bit):
    return u + bit * (1 - 2 * ((u // bit) % 2))


def flips(u, mask, top):
    bit = 1
    while bit < top:
        if mask & bit:
            u = flip(u, bit)
        bit *= 2
    return u


def kernel(sizes, rel_ref, col_ref, use_ref, h_ref, inc_ref, out_ref,
           inc_b, c00, c01, c10, c11, zh, xh0, xh1, h_t, acc, inc_v, own, in_s,
           zc_s, zc_r, zh_s, zh_r, xo_s, xo_r, xr_s, xr_r, xc_s, xc_r, tc_s, tc_r):
    S, T, rows, hw, qw, hs, qs, slots, nch, unroll, cpt = sizes
    p, t, m = lax.axis_index("section"), lax.axis_index("tp"), lax.axis_index("mirror")
    half = p // (S // 2)
    other = 1 - m
    hstart = (1 - half) * hs[0] + half * hs[1]
    hstart_there = half * hs[0] + (1 - half) * hs[1]
    qstart = pick(qs, half, m)
    qstart_there = pick(qs, half, other)
    partner = (p + S // 2) % S
    C = ((c00, c01), (c10, c11))

    def cols(start, n):
        return pl.ds(pl.multiple_of(start * BLK, BLK), n * BLK)

    mine = pl.ds(t * cpt, cpt)

    offsets = sorted({(sgn + s * (S // 2)) % S for sgn in (1, -1) for s in (0, 1)} | {S // 2})
    bits = []
    b = T // 2
    while b >= 1:
        bits.append(b)
        b //= 2
    peers = [{"section": (p + o) % S} for o in offsets] + [{"mirror": other}] + [{"tp": flip(t, b)} for b in bits]
    barrier = pltpu.get_barrier_semaphore()
    for peer in peers:
        pl.semaphore_signal(barrier, inc=1, device_id=peer, device_id_type=MESH)
    fetch_inc = pltpu.make_async_copy(inc_ref, inc_v, in_s.at[0])
    fetch_own = pltpu.make_async_copy(h_ref.at[:, :, cols(qstart, qw)], own, in_s.at[1])
    fetch_inc.start()
    fetch_own.start()
    fetch_inc.wait()
    for d in range(2):
        for c in range(cpt):
            inc_b[d, c] = inc_v[d, :, c * BLK:(c + 1) * BLK]
    pl.semaphore_wait(barrier, len(peers))

    def copy(src, dst, ss, rs, dev):
        return pltpu.make_async_remote_copy(
            src_ref=src, dst_ref=dst, send_sem=ss, recv_sem=rs, device_id=dev, device_id_type=MESH)

    zc = {}
    for s in range(2):
        for d in range(2):
            i = 2 * s + d
            dest = (p + (S - 1 if d == 0 else 1) + s * (S // 2)) % S
            zc[s, d] = copy(inc_b.at[d], C[s][0].at[d, mine], zc_s.at[i], zc_r.at[i], {"section": dest})
    per = nch // 2
    step = rows // per
    zhc, xr = [], []
    for i in range(nch):
        d, r = i // per, pl.ds((i % per) * step, step)
        zhc.append(copy(h_ref.at[d, r, cols(hstart_there, hw)], zh.at[d, r], zh_s.at[i], zh_r.at[i],
                        {"section": partner}))
        xr.append(copy(zh.at[d, r, cols(qstart_there - hstart, qw)], xh1.at[d, r], xr_s.at[i], xr_r.at[i],
                       {"mirror": other}))
    xo = [copy(h_ref.at[d, :, cols(qstart_there, qw)], xh0.at[d], xo_s.at[d], xo_r.at[d], {"mirror": other})
          for d in range(2)]
    xc = {}
    for s in range(2):
        for d in range(2):
            i = 2 * s + d
            xc[s, d] = copy(C[s][0].at[d, mine], C[s][1].at[d, mine], xc_s.at[i], xc_r.at[i], {"mirror": other})
    tc = {}
    stage_rels = []
    have = [0]
    for k, b in enumerate(bits):
        stage_rels.append(list(have))
        have = have + [r | b for r in have]
    for s in range(2):
        for d in range(2):
            for mr in range(2):
                n = ((s * 2 + d) * 2 + mr) * (T - 1)
                for k, b in enumerate(bits):
                    for r in stage_rels[k]:
                        u = flips(t, r, T)
                        ref = C[s][mr].at[d, pl.ds(u * cpt, cpt)]
                        tc[s, d, mr, k, r] = copy(ref, ref, tc_s.at[n], tc_r.at[n], {"tp": flip(t, b)})
                        n += 1

    def spread(s, d, mr, r, after):
        for k in range(after + 1, len(bits)):
            tc[s, d, mr, k, r].start()

    def stage_wait(s, mr, k):
        for d in range(2):
            for r in stage_rels[k]:
                tc[s, d, mr, k, r].wait_recv()
                spread(s, d, mr, r | bits[k], k)

    ahead = nch // 2

    def relay(i):
        zhc[i].wait_recv()
        xr[i].start()
        zhc[i].wait_send()
        if i + ahead < nch:
            zhc[i + ahead].start()

    def compute(lefts, rights, kind):
        def turn(b, carry):
            blk = jnp.concatenate([ref[d, :, cols(first + b, 1)] for ref, d, first in lefts], axis=0)
            h_t[b] = blk.T
            return carry

        lax.fori_loop(0, qw, turn, 0)

        def group(g, carry):
            for e in range(unroll):
                k = g * unroll + e
                right = jnp.concatenate([ref[d, col_ref[k]] for ref, d in rights], axis=0)
                got = jnp.dot(h_t[rel_ref[k]], right, preferred_element_type=jnp.float32)
                if kind != "first":
                    got = got + acc[k]
                if kind == "last":
                    out_ref[k] = (got * use_ref[k]).astype(out_ref.dtype)
                else:
                    acc[k] = got
            return carry

        lax.fori_loop(0, slots // unroll, group, 0)

    quarter = nch // 8

    def relays(g):
        for i in range(g * quarter, (g + 1) * quarter):
            relay(i)

    def start_hidden(g):
        for i in range(g * quarter, (g + 1) * quarter):
            zhc[i].start()

    last = len(bits) - 1
    for s in range(2):
        for d in range(2):
            zc[s, d].start()
    xo[0].start()
    start_hidden(0)
    for s in range(2):
        for d in range(2):
            zc[s, d].wait_recv()
            xc[s, d].start()
            spread(s, d, 0, 0, -1)
            if s == 0:
                zc[s, d].wait_send()
        start_hidden(s + 1)
    start_hidden(3)
    for s in range(2):
        for d in range(2):
            xc[s, d].wait_recv()
            spread(s, d, 1, 0, -1)
    xo[1].start()
    relays(0)
    for k in range(last):
        for mr in range(2):
            stage_wait(0, mr, k)
    relays(1)
    stage_wait(0, 0, last)
    fetch_own.wait()
    compute([(own, 0, 0), (own, 1, 0)], [(c00, 0), (c00, 1)], "first")
    relays(2)
    stage_wait(0, 1, last)
    for c in xo:
        c.wait_recv()
    compute([(xh0, 0, 0), (xh0, 1, 0)], [(c01, 0), (c01, 1)], "add")
    relays(3)
    for k in range(len(bits)):
        for mr in range(2):
            stage_wait(1, mr, k)
    relays(4)
    for c in xr[:per]:
        c.wait_recv()
    mid = qstart - hstart
    compute([(zh, 0, mid), (xh1, 0, 0)], [(c10, 0), (c11, 0)], "add")
    for g in range(5, 8):
        relays(g)
    for c in xr[per:]:
        c.wait_recv()
    compute([(zh, 1, mid), (xh1, 1, 0)], [(c10, 1), (c11, 1)], "last")
    zc[1, 0].wait_send()
    zc[1, 1].wait_send()
    for c in xo + list(xc.values()) + list(tc.values()) + xr:
        c.wait_send()


def body(hidden, incoming, block_mask):
    S, T = lax.axis_size("section"), lax.axis_size("tp")
    p, m = lax.axis_index("section"), lax.axis_index("mirror")
    _, ffb, db = block_mask.shape
    rows, ff, dm = hidden.shape[3], hidden.shape[4], incoming.shape[4]
    cap = ffb * db * 9 // 16
    slots = cap // 4
    hw, qw, hs, qs = windows(ffb, db)
    half = p // (S // 2)
    mask = lax.dynamic_index_in_dim(block_mask, p % (S // 2), 0, keepdims=False)
    running = jnp.cumsum(mask.reshape(-1))
    positions = (2 * half + m) * slots + jnp.arange(slots, dtype=jnp.int32)
    targets = jnp.sum((running[None, :] <= positions[:, None]).astype(jnp.int32), axis=1)
    use = (positions < running[-1]).astype(jnp.float32)
    targets = jnp.minimum(targets, ffb * db - 1)
    rel = jnp.clip(targets // db - pick(qs, half, m), 0, qw - 1)
    col = targets % db
    per_t = dm // BLK
    nch = 16
    unroll = max(u for u in range(1, 10) if slots % u == 0)
    sizes = (S, T, rows, hw, qw, hs, qs, slots, nch, unroll, per_t)
    bf = jnp.bfloat16
    vmem, smem = pl.BlockSpec(memory_space=pltpu.VMEM), pl.BlockSpec(memory_space=pltpu.SMEM)
    hbm = pl.BlockSpec(memory_space=pltpu.HBM)
    dma = pltpu.SemaphoreType.DMA
    n_tc = 8 * (T - 1)
    out = pl.pallas_call(
        functools.partial(kernel, sizes),
        out_shape=jax.ShapeDtypeStruct((slots, BLK, BLK), bf),
        in_specs=[smem] * 3 + [hbm] * 2,
        out_specs=vmem,
        scratch_shapes=[pltpu.VMEM((2, per_t, rows, BLK), bf)] + [pltpu.VMEM((2, db, rows, BLK), bf)] * 4
        + [pltpu.VMEM((2, rows, hw * BLK), bf)]
        + [pltpu.VMEM((2, rows, qw * BLK), bf)] * 2
        + [pltpu.VMEM((qw, BLK, 2 * rows), bf), pltpu.VMEM((slots, BLK, BLK), jnp.float32)]
        + [pltpu.VMEM((2, rows, dm), bf), pltpu.VMEM((2, rows, qw * BLK), bf), dma((2,))]
        + [dma((4,)), dma((4,)), dma((nch,)), dma((nch,)), dma((2,)), dma((2,)), dma((nch,)), dma((nch,)),
           dma((4,)), dma((4,)), dma((n_tc,)), dma((n_tc,))],
        compiler_params=pltpu.CompilerParams(
            collective_id=0, has_side_effects=True, vmem_limit_bytes=63 * 1024 * 1024),
        cost_estimate=pl.CostEstimate(
            flops=slots * BLK * BLK * rows * 16, bytes_accessed=8 * 1024 * 1024, transcendentals=0),
    )(rel.astype(jnp.int32), col.astype(jnp.int32), use,
      hidden.reshape(2, rows, ff), incoming.reshape(2, rows, dm))
    return out.reshape(1, 1, slots, BLK, BLK)


def solution(mesh):
    placed = (
        P(None, "section", "mirror", None, "tp"),
        P(None, "section", "mirror", None, "tp"),
        P(None, "tp", None),
    )
    return jax.shard_map(
        body,
        mesh=mesh,
        in_specs=placed,
        out_specs=P("section", "tp", "mirror", None, None),
        check_vma=False,
    )
```

```python
import functools

import jax
import jax.numpy as jnp
from jax import lax
from jax.experimental import pallas as pl
from jax.experimental.pallas import tpu as pltpu
from jax.sharding import PartitionSpec as P

BLK = 128
MESH = pl.DeviceIdType.MESH


def cdiv(a, b):
    return -(-a // b)


def windows(rows, cols):
    kept_min, cap = rows * cols * 7 // 16, rows * cols * 9 // 16

    def span(first, last):
        return first // cols, min(rows - 1, rows - max(1, cdiv(kept_min - last, cols)))

    halves = [span(h * cap // 2, (h + 1) * cap // 2 - 1) for h in range(2)]
    quarters = [span(q * cap // 4, (q + 1) * cap // 4 - 1) for q in range(4)]
    hw = max(b - a + 1 for a, b in halves)
    qw = max(b - a + 1 for a, b in quarters)
    hs = [min(a, rows - hw) for a, _ in halves]
    qs = [min(a, rows - qw) for a, _ in quarters]
    for q in range(4):
        h = q // 2
        qs[q] = max(hs[h], min(qs[q], hs[h] + hw - qw))
        assert qs[q] <= quarters[q][0] and qs[q] + qw > quarters[q][1]
        assert hs[h] <= halves[h][0] and hs[h] + hw > halves[h][1]
    return hw, qw, hs, qs


def pick(table, half, m):
    return (1 - half) * ((1 - m) * table[0] + m * table[1]) + half * ((1 - m) * table[2] + m * table[3])


def flip(u, bit):
    return u + bit * (1 - 2 * ((u // bit) % 2))


def flips(u, mask, top):
    bit = 1
    while bit < top:
        if mask & bit:
            u = flip(u, bit)
        bit *= 2
    return u


def slot_table(mask, first, qstart, qw, lanes):
    f, db = mask.shape
    kept = mask.astype(jnp.float32)

    def iota(shape, dim):
        return lax.broadcasted_iota(jnp.int32, shape, dim)

    upper = (iota((db, db), 0) <= iota((db, db), 1)).astype(jnp.float32)
    lower = (iota((f, f), 1) < iota((f, f), 0)).astype(jnp.float32)
    within = jnp.dot(kept, upper, preferred_element_type=jnp.float32)
    above = jnp.dot(lower, kept, preferred_element_type=jnp.float32)
    before = jnp.sum(above, axis=1, keepdims=True)
    end = before + jnp.sum(kept, axis=1, keepdims=True)
    pos = (first + iota((1, lanes), 1)).astype(jnp.float32)
    row = jnp.sum((end <= pos).astype(jnp.float32), axis=0, keepdims=True)
    hot = (iota((f, lanes), 0).astype(jnp.float32) == row).astype(jnp.float32)
    mine = pos - jnp.sum(hot * before, axis=0, keepdims=True)
    running = lax.dot_general(within, hot, (((0,), (0,)), ((), ())), preferred_element_type=jnp.float32)
    col = jnp.sum((running <= mine).astype(jnp.float32), axis=0, keepdims=True)
    use = (row < f).astype(jnp.int32)
    rel = jnp.clip(row.astype(jnp.int32) - qstart, 0, qw - 1)
    return rel, jnp.clip(col.astype(jnp.int32), 0, db - 1), use


def kernel(sizes, mask_ref, h_ref, inc_ref, out_ref,
           inc_b, c00, c01, c10, c11, zh, xh0, xh1, h_t, acc, inc_v, own, in_s, tab_v, tab,
           zc_s, zc_r, zh_s, zh_r, xo_s, xo_r, xr_s, xr_r, xc_s, xc_r, tc_s, tc_r):
    S, T, rows, hw, qw, hs, qs, slots, nch, unroll, cpt = sizes
    p, t, m = lax.axis_index("section"), lax.axis_index("tp"), lax.axis_index("mirror")
    half = p // (S // 2)
    other = 1 - m
    hstart = (1 - half) * hs[0] + half * hs[1]
    hstart_there = half * hs[0] + (1 - half) * hs[1]
    qstart = pick(qs, half, m)
    qstart_there = pick(qs, half, other)
    partner = (p + S // 2) % S
    C = ((c00, c01), (c10, c11))

    def cols(start, n):
        return pl.ds(pl.multiple_of(start * BLK, BLK), n * BLK)

    mine = pl.ds(t * cpt, cpt)

    offsets = sorted({(sgn + s * (S // 2)) % S for sgn in (1, -1) for s in (0, 1)} | {S // 2})
    bits = []
    b = T // 2
    while b >= 1:
        bits.append(b)
        b //= 2
    peers = [{"section": (p + o) % S} for o in offsets] + [{"mirror": other}] + [{"tp": flip(t, b)} for b in bits]
    barrier = pltpu.get_barrier_semaphore()
    for peer in peers:
        pl.semaphore_signal(barrier, inc=1, device_id=peer, device_id_type=MESH)
    fetch_inc = pltpu.make_async_copy(inc_ref, inc_v, in_s.at[0])
    fetch_own = pltpu.make_async_copy(h_ref.at[:, :, cols(qstart, qw)], own, in_s.at[1])
    fetch_inc.start()
    fetch_own.start()
    fetch_inc.wait()
    for d in range(2):
        for c in range(cpt):
            inc_b[d, c] = inc_v[d, :, c * BLK:(c + 1) * BLK]
    pl.semaphore_wait(barrier, len(peers))

    def copy(src, dst, ss, rs, dev):
        return pltpu.make_async_remote_copy(
            src_ref=src, dst_ref=dst, send_sem=ss, recv_sem=rs, device_id=dev, device_id_type=MESH)

    zc = {}
    for s in range(2):
        for d in range(2):
            i = 2 * s + d
            dest = (p + (S - 1 if d == 0 else 1) + s * (S // 2)) % S
            zc[s, d] = copy(inc_b.at[d], C[s][0].at[d, mine], zc_s.at[i], zc_r.at[i], {"section": dest})
    per = nch // 2
    step = rows // per
    zhc, xr = [], []
    for i in range(nch):
        d, r = i // per, pl.ds((i % per) * step, step)
        zhc.append(copy(h_ref.at[d, r, cols(hstart_there, hw)], zh.at[d, r], zh_s.at[i], zh_r.at[i],
                        {"section": partner}))
        xr.append(copy(zh.at[d, r, cols(qstart_there - hstart, qw)], xh1.at[d, r], xr_s.at[i], xr_r.at[i],
                       {"mirror": other}))
    xo = [copy(h_ref.at[d, :, cols(qstart_there, qw)], xh0.at[d], xo_s.at[d], xo_r.at[d], {"mirror": other})
          for d in range(2)]
    xc = {}
    for s in range(2):
        for d in range(2):
            i = 2 * s + d
            xc[s, d] = copy(C[s][0].at[d, mine], C[s][1].at[d, mine], xc_s.at[i], xc_r.at[i], {"mirror": other})
    tc = {}
    stage_rels = []
    have = [0]
    for k, b in enumerate(bits):
        stage_rels.append(list(have))
        have = have + [r | b for r in have]
    for s in range(2):
        for d in range(2):
            for mr in range(2):
                n = ((s * 2 + d) * 2 + mr) * (T - 1)
                for k, b in enumerate(bits):
                    for r in stage_rels[k]:
                        u = flips(t, r, T)
                        ref = C[s][mr].at[d, pl.ds(u * cpt, cpt)]
                        tc[s, d, mr, k, r] = copy(ref, ref, tc_s.at[n], tc_r.at[n], {"tp": flip(t, b)})
                        n += 1

    def spread(s, d, mr, r, after):
        for k in range(after + 1, len(bits)):
            tc[s, d, mr, k, r].start()

    def stage_wait(s, mr, k):
        for d in range(2):
            for r in stage_rels[k]:
                tc[s, d, mr, k, r].wait_recv()
                spread(s, d, mr, r | bits[k], k)

    ahead = nch // 2
    last_col = T * cpt - 1

    def relay(i):
        zhc[i].wait_recv()
        xr[i].start()
        zhc[i].wait_send()
        if i + ahead < nch:
            zhc[i + ahead].start()

    def compute(lefts, rights, kind):
        def turn(b, carry):
            blk = jnp.concatenate([ref[d, :, cols(first + b, 1)] for ref, d, first in lefts], axis=0)
            h_t[b] = blk.T
            return carry

        lax.fori_loop(0, qw, turn, 0)

        def group(g, carry):
            for e in range(unroll):
                k = g * unroll + e
                rel, col = jnp.clip(tab[0, k], 0, qw - 1), jnp.clip(tab[1, k], 0, last_col)
                right = jnp.concatenate([ref[d, col] for ref, d in rights], axis=0)
                got = jnp.dot(h_t[rel], right, preferred_element_type=jnp.float32)
                if kind != "first":
                    got = got + acc[k]
                if kind == "last":
                    out_ref[k] = (got * tab[2, k].astype(jnp.float32)).astype(out_ref.dtype)
                else:
                    acc[k] = got
            return carry

        lax.fori_loop(0, slots // unroll, group, 0)

    quarter = nch // 8

    def relays(g):
        for i in range(g * quarter, (g + 1) * quarter):
            relay(i)

    def start_hidden(g):
        for i in range(g * quarter, (g + 1) * quarter):
            zhc[i].start()

    last = len(bits) - 1
    for s in range(2):
        for d in range(2):
            zc[s, d].start()
    xo[0].start()
    start_hidden(0)
    rel, col, use = slot_table(mask_ref[p % (S // 2)], (2 * half + m) * slots, qstart, qw, tab_v.shape[1])
    tab_v[...] = jnp.zeros_like(tab_v)
    tab_v[0:1] = rel
    tab_v[1:2] = col
    tab_v[2:3] = use
    put_tab = pltpu.make_async_copy(tab_v, tab, in_s.at[2])
    put_tab.start()
    for s in range(2):
        for d in range(2):
            zc[s, d].wait_recv()
            xc[s, d].start()
            spread(s, d, 0, 0, -1)
            if s == 0:
                zc[s, d].wait_send()
        start_hidden(s + 1)
    start_hidden(3)
    for s in range(2):
        for d in range(2):
            xc[s, d].wait_recv()
            spread(s, d, 1, 0, -1)
    xo[1].start()
    relays(0)
    for k in range(last):
        for mr in range(2):
            stage_wait(0, mr, k)
    relays(1)
    stage_wait(0, 0, last)
    fetch_own.wait()
    put_tab.wait()
    compute([(own, 0, 0), (own, 1, 0)], [(c00, 0), (c00, 1)], "first")
    relays(2)
    stage_wait(0, 1, last)
    for c in xo:
        c.wait_recv()
    compute([(xh0, 0, 0), (xh0, 1, 0)], [(c01, 0), (c01, 1)], "add")
    relays(3)
    for k in range(len(bits)):
        for mr in range(2):
            stage_wait(1, mr, k)
    relays(4)
    for c in xr[:per]:
        c.wait_recv()
    mid = qstart - hstart
    compute([(zh, 0, mid), (xh1, 0, 0)], [(c10, 0), (c11, 0)], "add")
    for g in range(5, 8):
        relays(g)
    for c in xr[per:]:
        c.wait_recv()
    compute([(zh, 1, mid), (xh1, 1, 0)], [(c10, 1), (c11, 1)], "last")
    zc[1, 0].wait_send()
    zc[1, 1].wait_send()
    for c in xo + list(xc.values()) + list(tc.values()) + xr:
        c.wait_send()


def body(hidden, incoming, block_mask):
    S, T = lax.axis_size("section"), lax.axis_size("tp")
    _, ffb, db = block_mask.shape
    rows, ff, dm = hidden.shape[3], hidden.shape[4], incoming.shape[4]
    cap = ffb * db * 9 // 16
    slots = cap // 4
    hw, qw, hs, qs = windows(ffb, db)
    per_t = dm // BLK
    nch = 16
    unroll = max(u for u in range(1, 10) if slots % u == 0)
    sizes = (S, T, rows, hw, qw, hs, qs, slots, nch, unroll, per_t)
    bf = jnp.bfloat16
    lanes = cdiv(slots, BLK) * BLK
    vmem = pl.BlockSpec(memory_space=pltpu.VMEM)
    hbm = pl.BlockSpec(memory_space=pltpu.HBM)
    dma = pltpu.SemaphoreType.DMA
    n_tc = 8 * (T - 1)
    out = pl.pallas_call(
        functools.partial(kernel, sizes),
        out_shape=jax.ShapeDtypeStruct((slots, BLK, BLK), bf),
        in_specs=[vmem] + [hbm] * 2,
        out_specs=vmem,
        scratch_shapes=[pltpu.VMEM((2, per_t, rows, BLK), bf)] + [pltpu.VMEM((2, db, rows, BLK), bf)] * 4
        + [pltpu.VMEM((2, rows, hw * BLK), bf)]
        + [pltpu.VMEM((2, rows, qw * BLK), bf)] * 2
        + [pltpu.VMEM((qw, BLK, 2 * rows), bf), pltpu.VMEM((slots, BLK, BLK), jnp.float32)]
        + [pltpu.VMEM((2, rows, dm), bf), pltpu.VMEM((2, rows, qw * BLK), bf), dma((3,)),
           pltpu.VMEM((8, lanes), jnp.int32), pltpu.SMEM((8, lanes), jnp.int32)]
        + [dma((4,)), dma((4,)), dma((nch,)), dma((nch,)), dma((2,)), dma((2,)), dma((nch,)), dma((nch,)),
           dma((4,)), dma((4,)), dma((n_tc,)), dma((n_tc,))],
        compiler_params=pltpu.CompilerParams(
            collective_id=0, has_side_effects=True, vmem_limit_bytes=63 * 1024 * 1024),
        cost_estimate=pl.CostEstimate(
            flops=slots * BLK * BLK * rows * 16, bytes_accessed=8 * 1024 * 1024, transcendentals=0),
    )(block_mask,
      hidden.reshape(2, rows, ff), incoming.reshape(2, rows, dm))
    return out.reshape(1, 1, slots, BLK, BLK)


def solution(mesh):
    placed = (
        P(None, "section", "mirror", None, "tp"),
        P(None, "section", "mirror", None, "tp"),
        P(None, "tp", None),
    )
    return jax.shard_map(
        body,
        mesh=mesh,
        in_specs=placed,
        out_specs=P("section", "tp", "mirror", None, None),
        check_vma=False,
    )
```

```python
import functools

import jax
import jax.numpy as jnp
from jax import lax
from jax.experimental import pallas as pl
from jax.experimental.pallas import tpu as pltpu
from jax.sharding import PartitionSpec as P

BLK = 128
MESH = pl.DeviceIdType.MESH


def cdiv(a, b):
    return -(-a // b)


def windows(rows, cols):
    kept_min, cap = rows * cols * 7 // 16, rows * cols * 9 // 16

    def span(first, last):
        return first // cols, min(rows - 1, rows - max(1, cdiv(kept_min - last, cols)))

    halves = [span(h * cap // 2, (h + 1) * cap // 2 - 1) for h in range(2)]
    quarters = [span(q * cap // 4, (q + 1) * cap // 4 - 1) for q in range(4)]
    hw = max(b - a + 1 for a, b in halves)
    qw = max(b - a + 1 for a, b in quarters)
    hs = [min(a, rows - hw) for a, _ in halves]
    qs = [min(a, rows - qw) for a, _ in quarters]
    for q in range(4):
        h = q // 2
        qs[q] = max(hs[h], min(qs[q], hs[h] + hw - qw))
        assert qs[q] <= quarters[q][0] and qs[q] + qw > quarters[q][1]
        assert qs[q] - hs[h] in (0, hw - qw)
        assert hs[h] <= halves[h][0] and hs[h] + hw > halves[h][1]
    return hw, qw, hs, qs


def pick(table, half, m):
    return (1 - half) * ((1 - m) * table[0] + m * table[1]) + half * ((1 - m) * table[2] + m * table[3])


def flip(u, bit):
    return u + bit * (1 - 2 * ((u // bit) % 2))


def flips(u, mask, top):
    bit = 1
    while bit < top:
        if mask & bit:
            u = flip(u, bit)
        bit *= 2
    return u


def slot_table(mask, first, qstart, qw, lanes):
    f, db = mask.shape
    kept = mask.astype(jnp.float32)

    def iota(shape, dim):
        return lax.broadcasted_iota(jnp.int32, shape, dim)

    upper = (iota((db, db), 0) <= iota((db, db), 1)).astype(jnp.float32)
    lower = (iota((f, f), 1) < iota((f, f), 0)).astype(jnp.float32)
    within = jnp.dot(kept, upper, preferred_element_type=jnp.float32)
    above = jnp.dot(lower, kept, preferred_element_type=jnp.float32)
    before = jnp.sum(above, axis=1, keepdims=True)
    end = before + jnp.sum(kept, axis=1, keepdims=True)
    pos = (first + iota((1, lanes), 1)).astype(jnp.float32)
    row = jnp.sum((end <= pos).astype(jnp.float32), axis=0, keepdims=True)
    hot = (iota((f, lanes), 0).astype(jnp.float32) == row).astype(jnp.float32)
    mine = pos - jnp.sum(hot * before, axis=0, keepdims=True)
    running = lax.dot_general(within, hot, (((0,), (0,)), ((), ())), preferred_element_type=jnp.float32)
    col = jnp.sum((running <= mine).astype(jnp.float32), axis=0, keepdims=True)
    use = (row < f).astype(jnp.int32)
    rel = jnp.clip(row.astype(jnp.int32) - qstart, 0, qw - 1)
    return rel, jnp.clip(col.astype(jnp.int32), 0, db - 1), use


def kernel(sizes, mask_ref, h_ref, inc_ref, out_ref,
           inc_b, c00, c01, c10, c11, zh, xh0, xh1, h_t, acc, inc_v, own, in_s, tab_v, tab,
           zc_s, zc_r, zh_s, zh_r, xo_s, xo_r, xr_s, xr_r, xc_s, xc_r, tc_s, tc_r):
    S, T, rows, hw, qw, hs, qs, slots, nch, unroll, cpt = sizes
    p, t, m = lax.axis_index("section"), lax.axis_index("tp"), lax.axis_index("mirror")
    half = p // (S // 2)
    other = 1 - m
    hstart = (1 - half) * hs[0] + half * hs[1]
    hstart_there = half * hs[0] + (1 - half) * hs[1]
    qstart = pick(qs, half, m)
    qstart_there = pick(qs, half, other)
    partner = (p + S // 2) % S
    C = ((c00, c01), (c10, c11))

    def cols(start, n):
        return pl.ds(pl.multiple_of(start * BLK, BLK), n * BLK)

    mine = pl.ds(t * cpt, cpt)

    offsets = sorted({(sgn + s * (S // 2)) % S for sgn in (1, -1) for s in (0, 1)} | {S // 2})
    bits = []
    b = T // 2
    while b >= 1:
        bits.append(b)
        b //= 2
    peers = [{"section": (p + o) % S} for o in offsets] + [{"mirror": other}] + [{"tp": flip(t, b)} for b in bits]
    barrier = pltpu.get_barrier_semaphore()
    for peer in peers:
        pl.semaphore_signal(barrier, inc=1, device_id=peer, device_id_type=MESH)
    fetch_inc = pltpu.make_async_copy(inc_ref, inc_v, in_s.at[0])
    fetch_own = pltpu.make_async_copy(h_ref.at[:, :, cols(qstart, qw)], own, in_s.at[1])
    fetch_inc.start()
    fetch_own.start()
    fetch_inc.wait()
    for d in range(2):
        for c in range(cpt):
            inc_b[d, c] = inc_v[d, :, c * BLK:(c + 1) * BLK]
    pl.semaphore_wait(barrier, len(peers))

    def copy(src, dst, ss, rs, dev):
        return pltpu.make_async_remote_copy(
            src_ref=src, dst_ref=dst, send_sem=ss, recv_sem=rs, device_id=dev, device_id_type=MESH)

    zc = {}
    for s in range(2):
        for d in range(2):
            i = 2 * s + d
            dest = (p + (S - 1 if d == 0 else 1) + s * (S // 2)) % S
            zc[s, d] = copy(inc_b.at[d], C[s][0].at[d, mine], zc_s.at[i], zc_r.at[i], {"section": dest})
    per = nch // 2
    step = rows // per
    zhc, xr, relay_of = [], [], {}
    qstart_cross = pick(qs, 1 - half, other)
    spare = max(hw - qw, 1)

    def rest(start, base):
        return qw * (1 - (start - base) // spare)

    for i in range(nch):
        d, r = i // per, pl.ds((i % per) * step, step)
        zhc.append(copy(h_ref.at[d, r, cols(qstart_cross, qw)], zh.at[d, r, cols(qstart_cross - hstart_there, qw)],
                        zh_s.at[len(zhc)], zh_r.at[len(zhc)], {"section": partner}))
        xr.append(copy(zh.at[d, r, cols(qstart_there - hstart, qw)], xh1.at[d, r], xr_s.at[i], xr_r.at[i],
                       {"mirror": other}))
        relay_of[len(zhc) - 1] = xr[-1]
        if i % per == per - 1 and hw > qw:
            away = rest(qstart_cross, hstart_there)
            zhc.append(copy(h_ref.at[d, :, cols(hstart_there + away, hw - qw)], zh.at[d, :, cols(away, hw - qw)],
                            zh_s.at[len(zhc)], zh_r.at[len(zhc)], {"section": partner}))
    items = len(zhc)
    xo = [copy(h_ref.at[d, :, cols(qstart_there, qw)], xh0.at[d], xo_s.at[d], xo_r.at[d], {"mirror": other})
          for d in range(2)]
    xc = {}
    for s in range(2):
        for d in range(2):
            i = 2 * s + d
            xc[s, d] = copy(C[s][0].at[d, mine], C[s][1].at[d, mine], xc_s.at[i], xc_r.at[i], {"mirror": other})
    tc = {}
    stage_rels = []
    have = [0]
    for k, b in enumerate(bits):
        stage_rels.append(list(have))
        have = have + [r | b for r in have]
    for s in range(2):
        for d in range(2):
            for mr in range(2):
                n = ((s * 2 + d) * 2 + mr) * (T - 1)
                for k, b in enumerate(bits):
                    for r in stage_rels[k]:
                        u = flips(t, r, T)
                        ref = C[s][mr].at[d, pl.ds(u * cpt, cpt)]
                        tc[s, d, mr, k, r] = copy(ref, ref, tc_s.at[n], tc_r.at[n], {"tp": flip(t, b)})
                        n += 1

    def spread(s, d, mr, r, after):
        for k in range(after + 1, len(bits)):
            tc[s, d, mr, k, r].start()

    def stage_wait(s, mr, k):
        for d in range(2):
            for r in stage_rels[k]:
                tc[s, d, mr, k, r].wait_recv()
                spread(s, d, mr, r | bits[k], k)

    ahead = nch // 2
    last_col = T * cpt - 1

    def relay(i):
        zhc[i].wait_recv()
        if i in relay_of:
            relay_of[i].start()
        zhc[i].wait_send()
        if i + ahead < items:
            zhc[i + ahead].start()

    def compute(lefts, rights, kind):
        def turn(b, carry):
            blk = jnp.concatenate([ref[d, :, cols(first + b, 1)] for ref, d, first in lefts], axis=0)
            h_t[b] = blk.T
            return carry

        lax.fori_loop(0, qw, turn, 0)

        def group(g, carry):
            for e in range(unroll):
                k = g * unroll + e
                rel, col = jnp.clip(tab[0, k], 0, qw - 1), jnp.clip(tab[1, k], 0, last_col)
                right = jnp.concatenate([ref[d, col] for ref, d in rights], axis=0)
                got = jnp.dot(h_t[rel], right, preferred_element_type=jnp.float32)
                if kind != "first":
                    got = got + acc[k]
                if kind == "last":
                    out_ref[k] = (got * tab[2, k].astype(jnp.float32)).astype(out_ref.dtype)
                else:
                    acc[k] = got
            return carry

        lax.fori_loop(0, slots // unroll, group, 0)

    quarter = nch // 8
    done = [0]
    half_items = items // 2

    def relays(upto):
        for i in range(done[0], upto):
            relay(i)
        done[0] = upto

    def start_hidden(g):
        for i in range(g * quarter, (g + 1) * quarter):
            zhc[i].start()

    last = len(bits) - 1
    for s in range(2):
        for d in range(2):
            zc[s, d].start()
    xo[0].start()
    start_hidden(0)
    rel, col, use = slot_table(mask_ref[:, p % (S // 2)], (2 * half + m) * slots, qstart, qw, tab_v.shape[1])
    tab_v[...] = jnp.zeros_like(tab_v)
    tab_v[0:1] = rel
    tab_v[1:2] = col
    tab_v[2:3] = use
    put_tab = pltpu.make_async_copy(tab_v, tab, in_s.at[2])
    put_tab.start()
    for s in range(2):
        for d in range(2):
            zc[s, d].wait_recv()
            xc[s, d].start()
            spread(s, d, 0, 0, -1)
            if s == 0:
                zc[s, d].wait_send()
        start_hidden(s + 1)
    start_hidden(3)
    for s in range(2):
        for d in range(2):
            xc[s, d].wait_recv()
            spread(s, d, 1, 0, -1)
    xo[1].start()
    relays(quarter)
    for k in range(last):
        for mr in range(2):
            stage_wait(0, mr, k)
    relays(2 * quarter)
    stage_wait(0, 0, last)
    fetch_own.wait()
    put_tab.wait()
    compute([(own, 0, 0), (own, 1, 0)], [(c00, 0), (c00, 1)], "first")
    relays(3 * quarter)
    stage_wait(0, 1, last)
    for c in xo:
        c.wait_recv()
    compute([(xh0, 0, 0), (xh0, 1, 0)], [(c01, 0), (c01, 1)], "add")
    relays(half_items)
    for k in range(len(bits)):
        for mr in range(2):
            stage_wait(1, mr, k)
    relays(half_items + quarter)
    for c in xr[:per]:
        c.wait_recv()
    mid = qstart - hstart
    compute([(zh, 0, mid), (xh1, 0, 0)], [(c10, 0), (c11, 0)], "add")
    relays(items)
    for c in xr[per:]:
        c.wait_recv()
    compute([(zh, 1, mid), (xh1, 1, 0)], [(c10, 1), (c11, 1)], "last")
    zc[1, 0].wait_send()
    zc[1, 1].wait_send()
    for c in xo + list(xc.values()) + list(tc.values()) + xr:
        c.wait_send()


def body(hidden, incoming, block_mask):
    S, T = lax.axis_size("section"), lax.axis_size("tp")
    _, ffb, db = block_mask.shape
    rows, ff, dm = hidden.shape[3], hidden.shape[4], incoming.shape[4]
    cap = ffb * db * 9 // 16
    slots = cap // 4
    hw, qw, hs, qs = windows(ffb, db)
    per_t = dm // BLK
    nch = 16
    unroll = max(u for u in range(1, 22) if slots % u == 0)
    sizes = (S, T, rows, hw, qw, hs, qs, slots, nch, unroll, per_t)
    bf = jnp.bfloat16
    lanes = cdiv(slots, BLK) * BLK
    vmem = pl.BlockSpec(memory_space=pltpu.VMEM)
    hbm = pl.BlockSpec(memory_space=pltpu.HBM)
    dma = pltpu.SemaphoreType.DMA
    n_tc = 8 * (T - 1)
    out = pl.pallas_call(
        functools.partial(kernel, sizes),
        out_shape=jax.ShapeDtypeStruct((slots, BLK, BLK), bf),
        in_specs=[vmem] + [hbm] * 2,
        out_specs=vmem,
        scratch_shapes=[pltpu.VMEM((2, per_t, rows, BLK), bf)] + [pltpu.VMEM((2, db, rows, BLK), bf)] * 4
        + [pltpu.VMEM((2, rows, hw * BLK), bf)]
        + [pltpu.VMEM((2, rows, qw * BLK), bf)] * 2
        + [pltpu.VMEM((qw, BLK, 2 * rows), bf), pltpu.VMEM((slots, BLK, BLK), jnp.float32)]
        + [pltpu.VMEM((2, rows, dm), bf), pltpu.VMEM((2, rows, qw * BLK), bf), dma((3,)),
           pltpu.VMEM((8, lanes), jnp.int32), pltpu.SMEM((8, lanes), jnp.int32)]
        + [dma((4,)), dma((4,)), dma((nch + 2,)), dma((nch + 2,)), dma((2,)), dma((2,)), dma((nch,)), dma((nch,)),
           dma((4,)), dma((4,)), dma((n_tc,)), dma((n_tc,))],
        compiler_params=pltpu.CompilerParams(
            collective_id=0, has_side_effects=True, vmem_limit_bytes=63 * 1024 * 1024),
        cost_estimate=pl.CostEstimate(
            flops=slots * BLK * BLK * rows * 16, bytes_accessed=8 * 1024 * 1024, transcendentals=0),
    )(jnp.transpose(block_mask, (1, 0, 2)),
      hidden.reshape(2, rows, ff), incoming.reshape(2, rows, dm))
    return out.reshape(1, 1, slots, BLK, BLK)


def solution(mesh):
    placed = (
        P(None, "section", "mirror", None, "tp"),
        P(None, "section", "mirror", None, "tp"),
        P(None, "tp", None),
    )
    return jax.shard_map(
        body,
        mesh=mesh,
        in_specs=placed,
        out_specs=P("section", "tp", "mirror", None, None),
        check_vma=False,
    )
```

```python
import functools

import jax
import jax.numpy as jnp
from jax import lax
from jax.experimental import pallas as pl
from jax.experimental.pallas import tpu as pltpu
from jax.sharding import PartitionSpec as P

BLK = 128
MESH = pl.DeviceIdType.MESH


def cdiv(a, b):
    return -(-a // b)


def windows(rows, cols):
    kept_min, cap = rows * cols * 7 // 16, rows * cols * 9 // 16

    def span(first, last):
        return first // cols, min(rows - 1, rows - max(1, cdiv(kept_min - last, cols)))

    halves = [span(h * cap // 2, (h + 1) * cap // 2 - 1) for h in range(2)]
    quarters = [span(q * cap // 4, (q + 1) * cap // 4 - 1) for q in range(4)]
    hw = max(b - a + 1 for a, b in halves)
    qw = max(b - a + 1 for a, b in quarters)
    hs = [min(a, rows - hw) for a, _ in halves]
    qs = [min(a, rows - qw) for a, _ in quarters]
    for q in range(4):
        h = q // 2
        qs[q] = max(hs[h], min(qs[q], hs[h] + hw - qw))
        assert qs[q] <= quarters[q][0] and qs[q] + qw > quarters[q][1]
        assert qs[q] - hs[h] in (0, hw - qw)
        assert hs[h] <= halves[h][0] and hs[h] + hw > halves[h][1]
    return hw, qw, hs, qs


def pick(table, half, m):
    return (1 - half) * ((1 - m) * table[0] + m * table[1]) + half * ((1 - m) * table[2] + m * table[3])


def flip(u, bit):
    return u + bit * (1 - 2 * ((u // bit) % 2))


def flips(u, mask, top):
    bit = 1
    while bit < top:
        if mask & bit:
            u = flip(u, bit)
        bit *= 2
    return u


def slot_table(mask, first, qstart, qw, lanes):
    f, db = mask.shape
    kept = mask.astype(jnp.float32)

    def iota(shape, dim):
        return lax.broadcasted_iota(jnp.int32, shape, dim)

    upper = (iota((db, db), 0) <= iota((db, db), 1)).astype(jnp.float32)
    lower = (iota((f, f), 1) < iota((f, f), 0)).astype(jnp.float32)
    within = jnp.dot(kept, upper, preferred_element_type=jnp.float32)
    above = jnp.dot(lower, kept, preferred_element_type=jnp.float32)
    before = jnp.sum(above, axis=1, keepdims=True)
    end = before + jnp.sum(kept, axis=1, keepdims=True)
    pos = (first + iota((1, lanes), 1)).astype(jnp.float32)
    row = jnp.sum((end <= pos).astype(jnp.float32), axis=0, keepdims=True)
    hot = (iota((f, lanes), 0).astype(jnp.float32) == row).astype(jnp.float32)
    mine = pos - jnp.sum(hot * before, axis=0, keepdims=True)
    running = lax.dot_general(within, hot, (((0,), (0,)), ((), ())), preferred_element_type=jnp.float32)
    col = jnp.sum((running <= mine).astype(jnp.float32), axis=0, keepdims=True)
    use = (row < f).astype(jnp.int32)
    rel = jnp.clip(row.astype(jnp.int32) - qstart, 0, qw - 1)
    return rel, jnp.clip(col.astype(jnp.int32), 0, db - 1), use


def kernel(sizes, mask_ref, h_ref, inc_ref, acc_out, cot_out, turned_out, tab_out,
           inc_b, c00, c01, c10, c11, zh, xh0, xh1, h_t, acc, inc_v, own, in_s, tab_v, tab, out_s,
           zc_s, zc_r, zh_s, zh_r, xo_s, xo_r, xr_s, xr_r, xc_s, xc_r, tc_s, tc_r):
    S, T, rows, hw, qw, hs, qs, slots, nch, unroll, cpt = sizes
    p, t, m = lax.axis_index("section"), lax.axis_index("tp"), lax.axis_index("mirror")
    half = p // (S // 2)
    other = 1 - m
    hstart = (1 - half) * hs[0] + half * hs[1]
    hstart_there = half * hs[0] + (1 - half) * hs[1]
    qstart = pick(qs, half, m)
    qstart_there = pick(qs, half, other)
    partner = (p + S // 2) % S
    C = ((c00, c01), (c10, c11))

    def cols(start, n):
        return pl.ds(pl.multiple_of(start * BLK, BLK), n * BLK)

    mine = pl.ds(t * cpt, cpt)

    offsets = sorted({(sgn + s * (S // 2)) % S for sgn in (1, -1) for s in (0, 1)} | {S // 2})
    bits = []
    b = T // 2
    while b >= 1:
        bits.append(b)
        b //= 2
    peers = [{"section": (p + o) % S} for o in offsets] + [{"mirror": other}] + [{"tp": flip(t, b)} for b in bits]
    barrier = pltpu.get_barrier_semaphore()
    for peer in peers:
        pl.semaphore_signal(barrier, inc=1, device_id=peer, device_id_type=MESH)
    fetch_inc = pltpu.make_async_copy(inc_ref, inc_v, in_s.at[0])
    fetch_own = pltpu.make_async_copy(h_ref.at[:, :, cols(qstart, qw)], own, in_s.at[1])
    fetch_inc.start()
    fetch_own.start()
    pl.semaphore_wait(barrier, len(peers))

    def copy(src, dst, ss, rs, dev):
        return pltpu.make_async_remote_copy(
            src_ref=src, dst_ref=dst, send_sem=ss, recv_sem=rs, device_id=dev, device_id_type=MESH)

    zc = {}
    for s in range(2):
        for d in range(2):
            i = 2 * s + d
            dest = (p + (S - 1 if d == 0 else 1) + s * (S // 2)) % S
            zc[s, d] = copy(inc_b.at[d], C[s][0].at[d, mine], zc_s.at[i], zc_r.at[i], {"section": dest})
    per = nch // 2
    step = rows // per
    zhc, xr, relay_of = [], [], {}
    qstart_cross = pick(qs, 1 - half, other)
    spare = max(hw - qw, 1)

    def rest(start, base):
        return qw * (1 - (start - base) // spare)

    for i in range(nch):
        d, r = i // per, pl.ds((i % per) * step, step)
        zhc.append(copy(h_ref.at[d, r, cols(qstart_cross, qw)], zh.at[d, r, cols(qstart_cross - hstart_there, qw)],
                        zh_s.at[len(zhc)], zh_r.at[len(zhc)], {"section": partner}))
        xr.append(copy(zh.at[d, r, cols(qstart_there - hstart, qw)], xh1.at[d, r], xr_s.at[i], xr_r.at[i],
                       {"mirror": other}))
        relay_of[len(zhc) - 1] = xr[-1]
        if i % per == per - 1 and hw > qw:
            away = rest(qstart_cross, hstart_there)
            zhc.append(copy(h_ref.at[d, :, cols(hstart_there + away, hw - qw)], zh.at[d, :, cols(away, hw - qw)],
                            zh_s.at[len(zhc)], zh_r.at[len(zhc)], {"section": partner}))
    items = len(zhc)
    xo = [copy(h_ref.at[d, :, cols(qstart_there, qw)], xh0.at[d], xo_s.at[d], xo_r.at[d], {"mirror": other})
          for d in range(2)]
    xc = {}
    for s in range(2):
        for d in range(2):
            i = 2 * s + d
            xc[s, d] = copy(C[s][0].at[d, mine], C[s][1].at[d, mine], xc_s.at[i], xc_r.at[i], {"mirror": other})
    tc = {}
    stage_rels = []
    have = [0]
    for k, b in enumerate(bits):
        stage_rels.append(list(have))
        have = have + [r | b for r in have]
    for s in range(2):
        for d in range(2):
            for mr in range(2):
                n = ((s * 2 + d) * 2 + mr) * (T - 1)
                for k, b in enumerate(bits):
                    for r in stage_rels[k]:
                        u = flips(t, r, T)
                        ref = C[s][mr].at[d, pl.ds(u * cpt, cpt)]
                        tc[s, d, mr, k, r] = copy(ref, ref, tc_s.at[n], tc_r.at[n], {"tp": flip(t, b)})
                        n += 1

    def spread(s, d, mr, r, after):
        for k in range(after + 1, len(bits)):
            tc[s, d, mr, k, r].start()

    def stage_wait(s, mr, k):
        for d in range(2):
            for r in stage_rels[k]:
                tc[s, d, mr, k, r].wait_recv()
                spread(s, d, mr, r | bits[k], k)

    ahead = nch // 2
    last_col = T * cpt - 1

    def relay(i):
        zhc[i].wait_recv()
        if i in relay_of:
            relay_of[i].start()
        zhc[i].wait_send()
        if i + ahead < items:
            zhc[i + ahead].start()

    def turn_all(lefts):
        def turn(b, carry):
            blk = jnp.concatenate([ref[d, :, cols(first + b, 1)] for ref, d, first in lefts], axis=0)
            h_t[b] = blk.T
            return carry

        lax.fori_loop(0, qw, turn, 0)

    def compute(lefts, rights, kind):
        turn_all(lefts)

        def group(g, carry):
            for e in range(unroll):
                k = g * unroll + e
                rel, col = jnp.clip(tab[0, k], 0, qw - 1), jnp.clip(tab[1, k], 0, last_col)
                right = jnp.concatenate([ref[d, col] for ref, d in rights], axis=0)
                got = jnp.dot(h_t[rel], right, preferred_element_type=jnp.float32)
                if kind != "first":
                    got = got + acc[k]
                acc[k] = got
            return carry

        lax.fori_loop(0, slots // unroll, group, 0)

    quarter = nch // 8
    done = [0]
    half_items = items // 2

    def relays(upto):
        for i in range(done[0], upto):
            relay(i)
        done[0] = upto

    def start_hidden(g):
        for i in range(g * quarter, (g + 1) * quarter):
            zhc[i].start()

    last = len(bits) - 1
    zhc[0].start()
    xo[0].start()
    fetch_inc.wait()
    for d in range(2):
        for c in range(cpt):
            inc_b[d, c] = inc_v[d, :, c * BLK:(c + 1) * BLK]
    for s in range(2):
        for d in range(2):
            zc[s, d].start()
    for i in range(1, quarter):
        zhc[i].start()
    rel, col, use = slot_table(mask_ref[:, p % (S // 2)], (2 * half + m) * slots, qstart, qw, tab_v.shape[1])
    tab_v[...] = jnp.zeros_like(tab_v)
    tab_v[0:1] = rel
    tab_v[1:2] = col
    tab_v[2:3] = use
    put_tab = pltpu.make_async_copy(tab_v, tab, in_s.at[2])
    put_tab.start()
    for s in range(2):
        for d in range(2):
            zc[s, d].wait_recv()
            xc[s, d].start()
            spread(s, d, 0, 0, -1)
            if s == 0:
                zc[s, d].wait_send()
        start_hidden(s + 1)
    start_hidden(3)
    for s in range(2):
        for d in range(2):
            xc[s, d].wait_recv()
            spread(s, d, 1, 0, -1)
    xo[1].start()
    relays(quarter)
    for k in range(last):
        for mr in range(2):
            stage_wait(0, mr, k)
    relays(2 * quarter)
    stage_wait(0, 0, last)
    fetch_own.wait()
    put_tab.wait()
    compute([(own, 0, 0), (own, 1, 0)], [(c00, 0), (c00, 1)], "first")
    relays(3 * quarter)
    stage_wait(0, 1, last)
    for c in xo:
        c.wait_recv()
    compute([(xh0, 0, 0), (xh0, 1, 0)], [(c01, 0), (c01, 1)], "add")
    relays(half_items)
    for k in range(len(bits)):
        for mr in range(2):
            stage_wait(1, mr, k)
    relays(half_items + quarter)
    for c in xr[:per]:
        c.wait_recv()
    mid = qstart - hstart
    compute([(zh, 0, mid), (xh1, 0, 0)], [(c10, 0), (c11, 0)], "add")
    keep = [pltpu.make_async_copy(src, dst, out_s.at[i]) for i, (src, dst) in enumerate((
        (acc, acc_out), (c10.at[1], cot_out.at[0]), (c11.at[1], cot_out.at[1]), (tab_v, tab_out), (h_t, turned_out)))]
    for c in keep[:-1]:
        c.start()
    relays(items)
    for c in xr[per:]:
        c.wait_recv()
    turn_all([(zh, 1, mid), (xh1, 1, 0)])
    keep[-1].start()
    for c in keep:
        c.wait()
    zc[1, 0].wait_send()
    zc[1, 1].wait_send()
    for c in xo + list(xc.values()) + list(tc.values()) + xr:
        c.wait_send()


def last_pass(unroll, tab, turned, cot, acc, out):
    base = pl.program_id(0) * unroll
    qw, last_col = turned.shape[0], cot.shape[1] - 1
    for e in range(unroll):
        k = base + e
        rel, col = jnp.clip(tab[0, k], 0, qw - 1), jnp.clip(tab[1, k], 0, last_col)
        right = jnp.concatenate([cot[0, col], cot[1, col]], axis=0)
        got = acc[e] + jnp.dot(turned[rel], right, preferred_element_type=jnp.float32)
        out[e] = (got * tab[2, k].astype(jnp.float32)).astype(out.dtype)


def body(hidden, incoming, block_mask):
    S, T = lax.axis_size("section"), lax.axis_size("tp")
    _, ffb, db = block_mask.shape
    rows, ff, dm = hidden.shape[3], hidden.shape[4], incoming.shape[4]
    cap = ffb * db * 9 // 16
    slots = cap // 4
    hw, qw, hs, qs = windows(ffb, db)
    per_t = dm // BLK
    nch = 16
    unroll = max(u for u in range(1, 22) if slots % u == 0)
    sizes = (S, T, rows, hw, qw, hs, qs, slots, nch, unroll, per_t)
    bf = jnp.bfloat16
    lanes = cdiv(slots, BLK) * BLK
    vmem = pl.BlockSpec(memory_space=pltpu.VMEM)
    hbm = pl.BlockSpec(memory_space=pltpu.HBM)
    dma = pltpu.SemaphoreType.DMA
    n_tc = 8 * (T - 1)
    acc, cot, turned, tab = pl.pallas_call(
        functools.partial(kernel, sizes),
        out_shape=[
            jax.ShapeDtypeStruct((slots, BLK, BLK), jnp.float32),
            jax.ShapeDtypeStruct((2, db, rows, BLK), bf),
            jax.ShapeDtypeStruct((qw, BLK, 2 * rows), bf),
            jax.ShapeDtypeStruct((8, lanes), jnp.int32),
        ],
        in_specs=[vmem] + [hbm] * 2,
        out_specs=[hbm] * 4,
        scratch_shapes=[pltpu.VMEM((2, per_t, rows, BLK), bf)] + [pltpu.VMEM((2, db, rows, BLK), bf)] * 4
        + [pltpu.VMEM((2, rows, hw * BLK), bf)]
        + [pltpu.VMEM((2, rows, qw * BLK), bf)] * 2
        + [pltpu.VMEM((qw, BLK, 2 * rows), bf), pltpu.VMEM((slots, BLK, BLK), jnp.float32)]
        + [pltpu.VMEM((2, rows, dm), bf), pltpu.VMEM((2, rows, qw * BLK), bf), dma((3,)),
           pltpu.VMEM((8, lanes), jnp.int32), pltpu.SMEM((8, lanes), jnp.int32), dma((5,))]
        + [dma((4,)), dma((4,)), dma((nch + 2,)), dma((nch + 2,)), dma((2,)), dma((2,)), dma((nch,)), dma((nch,)),
           dma((4,)), dma((4,)), dma((n_tc,)), dma((n_tc,))],
        compiler_params=pltpu.CompilerParams(
            collective_id=0, has_side_effects=True, vmem_limit_bytes=63 * 1024 * 1024),
        cost_estimate=pl.CostEstimate(
            flops=slots * BLK * BLK * rows * 12, bytes_accessed=16 * 1024 * 1024, transcendentals=0),
    )(jnp.transpose(block_mask, (1, 0, 2)),
      hidden.reshape(2, rows, ff), incoming.reshape(2, rows, dm))
    per_step = pl.BlockSpec((unroll, BLK, BLK), lambda g: (g, 0, 0))
    out = pl.pallas_call(
        functools.partial(last_pass, unroll),
        grid=(slots // unroll,),
        out_shape=jax.ShapeDtypeStruct((slots, BLK, BLK), bf),
        in_specs=[pl.BlockSpec(memory_space=pltpu.SMEM), vmem, vmem, per_step],
        out_specs=per_step,
        compiler_params=pltpu.CompilerParams(vmem_limit_bytes=63 * 1024 * 1024),
        cost_estimate=pl.CostEstimate(
            flops=slots * BLK * BLK * rows * 4, bytes_accessed=16 * 1024 * 1024, transcendentals=0),
    )(tab, turned, cot, acc)
    return out.reshape(1, 1, slots, BLK, BLK)


def solution(mesh):
    placed = (
        P(None, "section", "mirror", None, "tp"),
        P(None, "section", "mirror", None, "tp"),
        P(None, "tp", None),
    )
    return jax.shard_map(
        body,
        mesh=mesh,
        in_specs=placed,
        out_specs=P("section", "tp", "mirror", None, None),
        check_vma=False,
    )
```

```python
import functools

import jax
import jax.numpy as jnp
from jax import lax
from jax.experimental import pallas as pl
from jax.experimental.pallas import tpu as pltpu
from jax.sharding import PartitionSpec as P

BLK = 128
MESH = pl.DeviceIdType.MESH


def cdiv(a, b):
    return -(-a // b)


def windows(rows, cols):
    kept_min, cap = rows * cols * 7 // 16, rows * cols * 9 // 16

    def span(first, last):
        return first // cols, min(rows - 1, rows - max(1, cdiv(kept_min - last, cols)))

    halves = [span(h * cap // 2, (h + 1) * cap // 2 - 1) for h in range(2)]
    quarters = [span(q * cap // 4, (q + 1) * cap // 4 - 1) for q in range(4)]
    hw = max(b - a + 1 for a, b in halves)
    qw = max(b - a + 1 for a, b in quarters)
    hs = [min(a, rows - hw) for a, _ in halves]
    qs = [min(a, rows - qw) for a, _ in quarters]
    for q in range(4):
        h = q // 2
        qs[q] = max(hs[h], min(qs[q], hs[h] + hw - qw))
        assert qs[q] <= quarters[q][0] and qs[q] + qw > quarters[q][1]
        assert qs[q] - hs[h] in (0, hw - qw)
        assert hs[h] <= halves[h][0] and hs[h] + hw > halves[h][1]
    return hw, qw, hs, qs


def pick(table, half, m):
    return (1 - half) * ((1 - m) * table[0] + m * table[1]) + half * ((1 - m) * table[2] + m * table[3])


def flip(u, bit):
    return u + bit * (1 - 2 * ((u // bit) % 2))


def flips(u, mask, top):
    bit = 1
    while bit < top:
        if mask & bit:
            u = flip(u, bit)
        bit *= 2
    return u


def slot_table(mask, first, qstart, qw, lanes):
    f, db = mask.shape
    kept = mask.astype(jnp.float32)

    def iota(shape, dim):
        return lax.broadcasted_iota(jnp.int32, shape, dim)

    upper = (iota((db, db), 0) <= iota((db, db), 1)).astype(jnp.float32)
    lower = (iota((f, f), 1) < iota((f, f), 0)).astype(jnp.float32)
    within = jnp.dot(kept, upper, preferred_element_type=jnp.float32)
    above = jnp.dot(lower, kept, preferred_element_type=jnp.float32)
    before = jnp.sum(above, axis=1, keepdims=True)
    end = before + jnp.sum(kept, axis=1, keepdims=True)
    pos = (first + iota((1, lanes), 1)).astype(jnp.float32)
    row = jnp.sum((end <= pos).astype(jnp.float32), axis=0, keepdims=True)
    hot = (iota((f, lanes), 0).astype(jnp.float32) == row).astype(jnp.float32)
    mine = pos - jnp.sum(hot * before, axis=0, keepdims=True)
    running = lax.dot_general(within, hot, (((0,), (0,)), ((), ())), preferred_element_type=jnp.float32)
    col = jnp.sum((running <= mine).astype(jnp.float32), axis=0, keepdims=True)
    use = (row < f).astype(jnp.int32)
    rel = jnp.clip(row.astype(jnp.int32) - qstart, 0, qw - 1)
    return rel, jnp.clip(col.astype(jnp.int32), 0, db - 1), use


def kernel(sizes, mask_ref, h_ref, inc_ref, out_ref,
           inc_b, c00, c01, c10, c11, zh, xh0, xh1, h_t, acc, inc_v, own, in_s, tab_v, tab, out_v, out_s,
           zc_s, zc_r, zh_s, zh_r, xo_s, xo_r, xr_s, xr_r, xc_s, xc_r, tc_s, tc_r):
    S, T, rows, hw, qw, hs, qs, slots, nch, unroll, cpt = sizes
    p, t, m = lax.axis_index("section"), lax.axis_index("tp"), lax.axis_index("mirror")
    half = p // (S // 2)
    other = 1 - m
    hstart = (1 - half) * hs[0] + half * hs[1]
    hstart_there = half * hs[0] + (1 - half) * hs[1]
    qstart = pick(qs, half, m)
    qstart_there = pick(qs, half, other)
    partner = (p + S // 2) % S
    C = ((c00, c01), (c10, c11))

    def cols(start, n):
        return pl.ds(pl.multiple_of(start * BLK, BLK), n * BLK)

    mine = pl.ds(t * cpt, cpt)

    offsets = sorted({(sgn + s * (S // 2)) % S for sgn in (1, -1) for s in (0, 1)} | {S // 2})
    bits = []
    b = T // 2
    while b >= 1:
        bits.append(b)
        b //= 2
    peers = [{"section": (p + o) % S} for o in offsets] + [{"mirror": other}] + [{"tp": flip(t, b)} for b in bits]
    barrier = pltpu.get_barrier_semaphore()
    for peer in peers:
        pl.semaphore_signal(barrier, inc=1, device_id=peer, device_id_type=MESH)
    fetch_inc = pltpu.make_async_copy(inc_ref, inc_v, in_s.at[0])
    fetch_own = pltpu.make_async_copy(h_ref.at[:, :, cols(qstart, qw)], own, in_s.at[1])
    fetch_inc.start()
    fetch_own.start()
    pl.semaphore_wait(barrier, len(peers))

    def copy(src, dst, ss, rs, dev):
        return pltpu.make_async_remote_copy(
            src_ref=src, dst_ref=dst, send_sem=ss, recv_sem=rs, device_id=dev, device_id_type=MESH)

    zc = {}
    for s in range(2):
        for d in range(2):
            i = 2 * s + d
            dest = (p + (S - 1 if d == 0 else 1) + s * (S // 2)) % S
            zc[s, d] = copy(inc_b.at[d], C[s][0].at[d, mine], zc_s.at[i], zc_r.at[i], {"section": dest})
    per = nch // 2
    step = rows // per
    zhc, xr, relay_of = [], [], {}
    qstart_cross = pick(qs, 1 - half, other)
    spare = max(hw - qw, 1)

    def rest(start, base):
        return qw * (1 - (start - base) // spare)

    for i in range(nch):
        d, r = i // per, pl.ds((i % per) * step, step)
        zhc.append(copy(h_ref.at[d, r, cols(qstart_cross, qw)], zh.at[d, r, cols(qstart_cross - hstart_there, qw)],
                        zh_s.at[len(zhc)], zh_r.at[len(zhc)], {"section": partner}))
        xr.append(copy(zh.at[d, r, cols(qstart_there - hstart, qw)], xh1.at[d, r], xr_s.at[i], xr_r.at[i],
                       {"mirror": other}))
        relay_of[len(zhc) - 1] = xr[-1]
        if i % per == per - 1 and hw > qw:
            away = rest(qstart_cross, hstart_there)
            zhc.append(copy(h_ref.at[d, :, cols(hstart_there + away, hw - qw)], zh.at[d, :, cols(away, hw - qw)],
                            zh_s.at[len(zhc)], zh_r.at[len(zhc)], {"section": partner}))
    items = len(zhc)
    xo = [copy(h_ref.at[d, :, cols(qstart_there, qw)], xh0.at[d], xo_s.at[d], xo_r.at[d], {"mirror": other})
          for d in range(2)]
    xc = {}
    for s in range(2):
        for d in range(2):
            i = 2 * s + d
            xc[s, d] = copy(C[s][0].at[d, mine], C[s][1].at[d, mine], xc_s.at[i], xc_r.at[i], {"mirror": other})
    tc = {}
    stage_rels = []
    have = [0]
    for k, b in enumerate(bits):
        stage_rels.append(list(have))
        have = have + [r | b for r in have]
    for s in range(2):
        for d in range(2):
            for mr in range(2):
                n = ((s * 2 + d) * 2 + mr) * (T - 1)
                for k, b in enumerate(bits):
                    for r in stage_rels[k]:
                        u = flips(t, r, T)
                        ref = C[s][mr].at[d, pl.ds(u * cpt, cpt)]
                        tc[s, d, mr, k, r] = copy(ref, ref, tc_s.at[n], tc_r.at[n], {"tp": flip(t, b)})
                        n += 1

    def spread(s, d, mr, r, after):
        for k in range(after + 1, len(bits)):
            tc[s, d, mr, k, r].start()

    def stage_wait(s, mr, k):
        for d in range(2):
            for r in stage_rels[k]:
                tc[s, d, mr, k, r].wait_recv()
                spread(s, d, mr, r | bits[k], k)

    ahead = nch // 2
    last_col = T * cpt - 1

    def relay(i):
        zhc[i].wait_recv()
        if i in relay_of:
            relay_of[i].start()
        zhc[i].wait_send()
        if i + ahead < items:
            zhc[i + ahead].start()

    def put(g):
        part = pl.ds(g * unroll, unroll)
        return pltpu.make_async_copy(out_v.at[part], out_ref.at[part], out_s.at[g])

    def compute(lefts, rights, kind):
        def turn(b, carry):
            blk = jnp.concatenate([ref[d, :, cols(first + b, 1)] for ref, d, first in lefts], axis=0)
            h_t[b] = blk.T
            return carry

        lax.fori_loop(0, qw, turn, 0)

        def group(g, carry):
            for e in range(unroll):
                k = g * unroll + e
                rel, col = jnp.clip(tab[0, k], 0, qw - 1), jnp.clip(tab[1, k], 0, last_col)
                right = jnp.concatenate([ref[d, col] for ref, d in rights], axis=0)
                got = jnp.dot(h_t[rel], right, preferred_element_type=jnp.float32)
                if kind != "first":
                    got = got + acc[k]
                if kind == "last":
                    out_v[k] = (got * tab[2, k].astype(jnp.float32)).astype(out_v.dtype)
                else:
                    acc[k] = got
            if kind == "last":
                put(g).start()
            return carry

        lax.fori_loop(0, slots // unroll, group, 0)

    quarter = nch // 8
    done = [0]
    half_items = items // 2

    def relays(upto):
        for i in range(done[0], upto):
            relay(i)
        done[0] = upto

    def start_hidden(g):
        for i in range(g * quarter, (g + 1) * quarter):
            zhc[i].start()

    last = len(bits) - 1
    zhc[0].start()
    xo[0].start()
    fetch_inc.wait()
    for d in range(2):
        for c in range(cpt):
            inc_b[d, c] = inc_v[d, :, c * BLK:(c + 1) * BLK]
    for s in range(2):
        for d in range(2):
            zc[s, d].start()
    for i in range(1, quarter):
        zhc[i].start()
    rel, col, use = slot_table(mask_ref[:, p % (S // 2)], (2 * half + m) * slots, qstart, qw, tab_v.shape[1])
    tab_v[...] = jnp.zeros_like(tab_v)
    tab_v[0:1] = rel
    tab_v[1:2] = col
    tab_v[2:3] = use
    put_tab = pltpu.make_async_copy(tab_v, tab, in_s.at[2])
    put_tab.start()
    for s in range(2):
        for d in range(2):
            zc[s, d].wait_recv()
            xc[s, d].start()
            spread(s, d, 0, 0, -1)
            if s == 0:
                zc[s, d].wait_send()
        start_hidden(s + 1)
    start_hidden(3)
    for s in range(2):
        for d in range(2):
            xc[s, d].wait_recv()
            spread(s, d, 1, 0, -1)
    xo[1].start()
    relays(quarter)
    for k in range(last):
        for mr in range(2):
            stage_wait(0, mr, k)
    relays(2 * quarter)
    stage_wait(0, 0, last)
    fetch_own.wait()
    put_tab.wait()
    compute([(own, 0, 0), (own, 1, 0)], [(c00, 0), (c00, 1)], "first")
    relays(3 * quarter)
    stage_wait(0, 1, last)
    for c in xo:
        c.wait_recv()
    compute([(xh0, 0, 0), (xh0, 1, 0)], [(c01, 0), (c01, 1)], "add")
    relays(half_items)
    for k in range(len(bits)):
        for mr in range(2):
            stage_wait(1, mr, k)
    relays(half_items + quarter)
    for c in xr[:per]:
        c.wait_recv()
    mid = qstart - hstart
    compute([(zh, 0, mid), (xh1, 0, 0)], [(c10, 0), (c11, 0)], "add")
    relays(items)
    for c in xr[per:]:
        c.wait_recv()
    compute([(zh, 1, mid), (xh1, 1, 0)], [(c10, 1), (c11, 1)], "last")
    for g in range(slots // unroll):
        put(g).wait()
    zc[1, 0].wait_send()
    zc[1, 1].wait_send()
    for c in xo + list(xc.values()) + list(tc.values()) + xr:
        c.wait_send()


def hand_over(src, dst):
    dst[...] = src[...]


def body(hidden, incoming, block_mask):
    S, T = lax.axis_size("section"), lax.axis_size("tp")
    _, ffb, db = block_mask.shape
    rows, ff, dm = hidden.shape[3], hidden.shape[4], incoming.shape[4]
    cap = ffb * db * 9 // 16
    slots = cap // 4
    hw, qw, hs, qs = windows(ffb, db)
    per_t = dm // BLK
    nch = 16
    unroll = max(u for u in range(1, 22) if slots % u == 0)
    sizes = (S, T, rows, hw, qw, hs, qs, slots, nch, unroll, per_t)
    bf = jnp.bfloat16
    lanes = cdiv(slots, BLK) * BLK
    vmem = pl.BlockSpec(memory_space=pltpu.VMEM)
    hbm = pl.BlockSpec(memory_space=pltpu.HBM)
    dma = pltpu.SemaphoreType.DMA
    n_tc = 8 * (T - 1)
    out = pl.pallas_call(
        functools.partial(kernel, sizes),
        out_shape=jax.ShapeDtypeStruct((slots, BLK, BLK), bf),
        in_specs=[vmem] + [hbm] * 2,
        out_specs=hbm,
        scratch_shapes=[pltpu.VMEM((2, per_t, rows, BLK), bf)] + [pltpu.VMEM((2, db, rows, BLK), bf)] * 4
        + [pltpu.VMEM((2, rows, hw * BLK), bf)]
        + [pltpu.VMEM((2, rows, qw * BLK), bf)] * 2
        + [pltpu.VMEM((qw, BLK, 2 * rows), bf), pltpu.VMEM((slots, BLK, BLK), jnp.float32)]
        + [pltpu.VMEM((2, rows, dm), bf), pltpu.VMEM((2, rows, qw * BLK), bf), dma((3,)),
           pltpu.VMEM((8, lanes), jnp.int32), pltpu.SMEM((8, lanes), jnp.int32),
           pltpu.VMEM((slots, BLK, BLK), bf), dma((slots // unroll,))]
        + [dma((4,)), dma((4,)), dma((nch + 2,)), dma((nch + 2,)), dma((2,)), dma((2,)), dma((nch,)), dma((nch,)),
           dma((4,)), dma((4,)), dma((n_tc,)), dma((n_tc,))],
        compiler_params=pltpu.CompilerParams(
            collective_id=0, has_side_effects=True, vmem_limit_bytes=63 * 1024 * 1024),
        cost_estimate=pl.CostEstimate(
            flops=slots * BLK * BLK * rows * 16, bytes_accessed=8 * 1024 * 1024, transcendentals=0),
    )(jnp.transpose(block_mask, (1, 0, 2)),
      hidden.reshape(2, rows, ff), incoming.reshape(2, rows, dm))
    part = pl.BlockSpec((unroll, BLK, BLK), lambda g: (g, 0, 0))
    out = pl.pallas_call(
        hand_over,
        grid=(slots // unroll,),
        out_shape=jax.ShapeDtypeStruct((slots, BLK, BLK), bf),
        in_specs=[part],
        out_specs=part,
        compiler_params=pltpu.CompilerParams(vmem_limit_bytes=63 * 1024 * 1024),
    )(out)
    return out.reshape(1, 1, slots, BLK, BLK)


def solution(mesh):
    placed = (
        P(None, "section", "mirror", None, "tp"),
        P(None, "section", "mirror", None, "tp"),
        P(None, "tp", None),
    )
    return jax.shard_map(
        body,
        mesh=mesh,
        in_specs=placed,
        out_specs=P("section", "tp", "mirror", None, None),
        check_vma=False,
    )
```

```python
import functools

import jax
import jax.numpy as jnp
from jax import lax
from jax.experimental import pallas as pl
from jax.experimental.pallas import tpu as pltpu
from jax.sharding import PartitionSpec as P

BLK = 128
MESH = pl.DeviceIdType.MESH


def cdiv(a, b):
    return -(-a // b)


def windows(rows, cols):
    kept_min, cap = rows * cols * 7 // 16, rows * cols * 9 // 16

    def span(first, last):
        return first // cols, min(rows - 1, rows - max(1, cdiv(kept_min - last, cols)))

    halves = [span(h * cap // 2, (h + 1) * cap // 2 - 1) for h in range(2)]
    quarters = [span(q * cap // 4, (q + 1) * cap // 4 - 1) for q in range(4)]
    hw = max(b - a + 1 for a, b in halves)
    qw = max(b - a + 1 for a, b in quarters)
    hs = [min(a, rows - hw) for a, _ in halves]
    qs = [min(a, rows - qw) for a, _ in quarters]
    for q in range(4):
        h = q // 2
        qs[q] = max(hs[h], min(qs[q], hs[h] + hw - qw))
        assert qs[q] <= quarters[q][0] and qs[q] + qw > quarters[q][1]
        assert qs[q] - hs[h] in (0, hw - qw)
        assert hs[h] <= halves[h][0] and hs[h] + hw > halves[h][1]
    return hw, qw, hs, qs


def pick(table, half, m):
    return (1 - half) * ((1 - m) * table[0] + m * table[1]) + half * ((1 - m) * table[2] + m * table[3])


def flip(u, bit):
    return u + bit * (1 - 2 * ((u // bit) % 2))


def flips(u, mask, top):
    bit = 1
    while bit < top:
        if mask & bit:
            u = flip(u, bit)
        bit *= 2
    return u


def slot_table(mask, first, qstart, qw, lanes):
    f, db = mask.shape
    kept = mask.astype(jnp.float32)

    def iota(shape, dim):
        return lax.broadcasted_iota(jnp.int32, shape, dim)

    upper = (iota((db, db), 0) <= iota((db, db), 1)).astype(jnp.float32)
    lower = (iota((f, f), 1) < iota((f, f), 0)).astype(jnp.float32)
    within = jnp.dot(kept, upper, preferred_element_type=jnp.float32)
    above = jnp.dot(lower, kept, preferred_element_type=jnp.float32)
    before = jnp.sum(above, axis=1, keepdims=True)
    end = before + jnp.sum(kept, axis=1, keepdims=True)
    pos = (first + iota((1, lanes), 1)).astype(jnp.float32)
    row = jnp.sum((end <= pos).astype(jnp.float32), axis=0, keepdims=True)
    hot = (iota((f, lanes), 0).astype(jnp.float32) == row).astype(jnp.float32)
    mine = pos - jnp.sum(hot * before, axis=0, keepdims=True)
    running = lax.dot_general(within, hot, (((0,), (0,)), ((), ())), preferred_element_type=jnp.float32)
    col = jnp.sum((running <= mine).astype(jnp.float32), axis=0, keepdims=True)
    use = (row < f).astype(jnp.int32)
    rel = jnp.clip(row.astype(jnp.int32) - qstart, 0, qw - 1)
    return rel, jnp.clip(col.astype(jnp.int32), 0, db - 1), use


def kernel(sizes, mask_ref, h_ref, inc_ref, acc_out, cot_out, turned_out, tab_out,
           inc_b, c00, c01, c10, c11, zh, xh0, xh1, h_t, acc, inc_v, own, in_s, tab_v, tab, out_s,
           zc_s, zc_r, zh_s, zh_r, xo_s, xo_r, xr_s, xr_r, xc_s, xc_r, tc_s, tc_r):
    S, T, rows, hw, qw, hs, qs, slots, nch, unroll, cpt = sizes
    p, t, m = lax.axis_index("section"), lax.axis_index("tp"), lax.axis_index("mirror")
    half = p // (S // 2)
    other = 1 - m
    hstart = (1 - half) * hs[0] + half * hs[1]
    hstart_there = half * hs[0] + (1 - half) * hs[1]
    qstart = pick(qs, half, m)
    qstart_there = pick(qs, half, other)
    partner = (p + S // 2) % S
    C = ((c00, c01), (c10, c11))

    def cols(start, n):
        return pl.ds(pl.multiple_of(start * BLK, BLK), n * BLK)

    mine = pl.ds(t * cpt, cpt)

    offsets = sorted({(sgn + s * (S // 2)) % S for sgn in (1, -1) for s in (0, 1)} | {S // 2})
    bits = []
    b = T // 2
    while b >= 1:
        bits.append(b)
        b //= 2
    peers = [{"section": (p + o) % S} for o in offsets] + [{"mirror": other}] + [{"tp": flip(t, b)} for b in bits]
    barrier = pltpu.get_barrier_semaphore()
    for peer in peers:
        pl.semaphore_signal(barrier, inc=1, device_id=peer, device_id_type=MESH)
    fetch_inc = pltpu.make_async_copy(inc_ref, inc_v, in_s.at[0])
    fetch_own = pltpu.make_async_copy(h_ref.at[:, :, cols(qstart, qw)], own, in_s.at[1])
    fetch_inc.start()
    fetch_own.start()
    pl.semaphore_wait(barrier, len(peers))

    def copy(src, dst, ss, rs, dev):
        return pltpu.make_async_remote_copy(
            src_ref=src, dst_ref=dst, send_sem=ss, recv_sem=rs, device_id=dev, device_id_type=MESH)

    zc = {}
    for s in range(2):
        for d in range(2):
            i = 2 * s + d
            dest = (p + (S - 1 if d == 0 else 1) + s * (S // 2)) % S
            zc[s, d] = copy(inc_b.at[d], C[s][0].at[d, mine], zc_s.at[i], zc_r.at[i], {"section": dest})
    per = nch // 2
    step = rows // per
    zhc, xr, relay_of = [], [], {}
    qstart_cross = pick(qs, 1 - half, other)
    spare = max(hw - qw, 1)

    def rest(start, base):
        return qw * (1 - (start - base) // spare)

    for i in range(nch):
        d, r = i // per, pl.ds((i % per) * step, step)
        zhc.append(copy(h_ref.at[d, r, cols(qstart_cross, qw)], zh.at[d, r, cols(qstart_cross - hstart_there, qw)],
                        zh_s.at[len(zhc)], zh_r.at[len(zhc)], {"section": partner}))
        xr.append(copy(zh.at[d, r, cols(qstart_there - hstart, qw)], xh1.at[d, r], xr_s.at[i], xr_r.at[i],
                       {"mirror": other}))
        relay_of[len(zhc) - 1] = xr[-1]
        if i % per == per - 1 and hw > qw:
            away = rest(qstart_cross, hstart_there)
            zhc.append(copy(h_ref.at[d, :, cols(hstart_there + away, hw - qw)], zh.at[d, :, cols(away, hw - qw)],
                            zh_s.at[len(zhc)], zh_r.at[len(zhc)], {"section": partner}))
    items = len(zhc)
    xo = [copy(h_ref.at[d, :, cols(qstart_there, qw)], xh0.at[d], xo_s.at[d], xo_r.at[d], {"mirror": other})
          for d in range(2)]
    xc = {}
    for s in range(2):
        for d in range(2):
            i = 2 * s + d
            xc[s, d] = copy(C[s][0].at[d, mine], C[s][1].at[d, mine], xc_s.at[i], xc_r.at[i], {"mirror": other})
    tc = {}
    stage_rels = []
    have = [0]
    for k, b in enumerate(bits):
        stage_rels.append(list(have))
        have = have + [r | b for r in have]
    for s in range(2):
        for d in range(2):
            for mr in range(2):
                n = ((s * 2 + d) * 2 + mr) * (T - 1)
                for k, b in enumerate(bits):
                    for r in stage_rels[k]:
                        u = flips(t, r, T)
                        ref = C[s][mr].at[d, pl.ds(u * cpt, cpt)]
                        tc[s, d, mr, k, r] = copy(ref, ref, tc_s.at[n], tc_r.at[n], {"tp": flip(t, b)})
                        n += 1

    def spread(s, d, mr, r, after):
        for k in range(after + 1, len(bits)):
            tc[s, d, mr, k, r].start()

    def stage_wait(s, mr, k):
        for d in range(2):
            for r in stage_rels[k]:
                tc[s, d, mr, k, r].wait_recv()
                spread(s, d, mr, r | bits[k], k)

    ahead = nch // 2
    last_col = T * cpt - 1

    def relay(i):
        zhc[i].wait_recv()
        if i in relay_of:
            relay_of[i].start()
        zhc[i].wait_send()
        if i + ahead < items:
            zhc[i + ahead].start()

    def turn_all(lefts):
        def turn(b, carry):
            blk = jnp.concatenate([ref[d, :, cols(first + b, 1)] for ref, d, first in lefts], axis=0)
            h_t[b] = blk.T
            return carry

        lax.fori_loop(0, qw, turn, 0)

    def compute(lefts, rights, kind):
        turn_all(lefts)

        def group(g, carry):
            for e in range(unroll):
                k = g * unroll + e
                rel, col = jnp.clip(tab[0, k], 0, qw - 1), jnp.clip(tab[1, k], 0, last_col)
                right = jnp.concatenate([ref[d, col] for ref, d in rights], axis=0)
                got = jnp.dot(h_t[rel], right, preferred_element_type=jnp.float32)
                if kind != "first":
                    got = got + acc[k]
                acc[k] = got
            return carry

        lax.fori_loop(0, slots // unroll, group, 0)

    quarter = nch // 8
    done = [0]
    half_items = items // 2

    def relays(upto):
        for i in range(done[0], upto):
            relay(i)
        done[0] = upto

    def start_hidden(g):
        for i in range(g * quarter, (g + 1) * quarter):
            zhc[i].start()

    last = len(bits) - 1
    zhc[0].start()
    xo[0].start()
    fetch_inc.wait()
    for d in range(2):
        for c in range(cpt):
            inc_b[d, c] = inc_v[d, :, c * BLK:(c + 1) * BLK]
    for s in range(2):
        for d in range(2):
            zc[s, d].start()
    for i in range(1, quarter):
        zhc[i].start()
    rel, col, use = slot_table(mask_ref[:, p % (S // 2)], (2 * half + m) * slots, qstart, qw, tab_v.shape[1])
    tab_v[...] = jnp.zeros_like(tab_v)
    tab_v[0:1] = rel
    tab_v[1:2] = col
    tab_v[2:3] = use
    put_tab = pltpu.make_async_copy(tab_v, tab, in_s.at[2])
    put_tab.start()
    for s in range(2):
        for d in range(2):
            zc[s, d].wait_recv()
            xc[s, d].start()
            spread(s, d, 0, 0, -1)
            if s == 0:
                zc[s, d].wait_send()
        start_hidden(s + 1)
    start_hidden(3)
    for s in range(2):
        for d in range(2):
            xc[s, d].wait_recv()
            spread(s, d, 1, 0, -1)
    xo[1].start()
    relays(quarter)
    for k in range(last):
        for mr in range(2):
            stage_wait(0, mr, k)
    relays(2 * quarter)
    stage_wait(0, 0, last)
    fetch_own.wait()
    put_tab.wait()
    compute([(own, 0, 0), (own, 1, 0)], [(c00, 0), (c00, 1)], "first")
    relays(3 * quarter)
    stage_wait(0, 1, last)
    for c in xo:
        c.wait_recv()
    compute([(xh0, 0, 0), (xh0, 1, 0)], [(c01, 0), (c01, 1)], "add")
    relays(half_items)
    for k in range(len(bits)):
        for mr in range(2):
            stage_wait(1, mr, k)
    relays(half_items + quarter)
    for c in xr[:per]:
        c.wait_recv()
    mid = qstart - hstart
    compute([(zh, 0, mid), (xh1, 0, 0)], [(c10, 0), (c11, 0)], "add")
    keep = [pltpu.make_async_copy(src, dst, out_s.at[i]) for i, (src, dst) in enumerate((
        (acc, acc_out), (c10.at[1], cot_out.at[0]), (c11.at[1], cot_out.at[1]), (tab_v, tab_out), (h_t, turned_out)))]
    for c in keep[:-1]:
        c.start()
    relays(items)
    for c in xr[per:]:
        c.wait_recv()
    turn_all([(zh, 1, mid), (xh1, 1, 0)])
    keep[-1].start()
    for c in keep:
        c.wait()
    zc[1, 0].wait_send()
    zc[1, 1].wait_send()
    for c in xo + list(xc.values()) + list(tc.values()) + xr:
        c.wait_send()


def last_pass(unroll, tab, turned, cot, acc, out):
    base = pl.program_id(0) * unroll
    qw, last_col = turned.shape[0], cot.shape[1] - 1
    for e in range(unroll):
        k = base + e
        rel, col = jnp.clip(tab[0, k], 0, qw - 1), jnp.clip(tab[1, k], 0, last_col)
        right = jnp.concatenate([cot[0, col], cot[1, col]], axis=0)
        got = acc[e] + jnp.dot(turned[rel], right, preferred_element_type=jnp.float32)
        out[e] = (got * tab[2, k].astype(jnp.float32)).astype(out.dtype)


def body(hidden, incoming, block_mask):
    S, T = lax.axis_size("section"), lax.axis_size("tp")
    _, ffb, db = block_mask.shape
    rows, ff, dm = hidden.shape[3], hidden.shape[4], incoming.shape[4]
    cap = ffb * db * 9 // 16
    slots = cap // 4
    hw, qw, hs, qs = windows(ffb, db)
    per_t = dm // BLK
    nch = 16
    unroll = max(u for u in range(1, 22) if slots % u == 0)
    sizes = (S, T, rows, hw, qw, hs, qs, slots, nch, unroll, per_t)
    bf = jnp.bfloat16
    lanes = cdiv(slots, BLK) * BLK
    vmem = pl.BlockSpec(memory_space=pltpu.VMEM)
    hbm = pl.BlockSpec(memory_space=pltpu.HBM)
    dma = pltpu.SemaphoreType.DMA
    n_tc = 8 * (T - 1)
    acc, cot, turned, tab = pl.pallas_call(
        functools.partial(kernel, sizes),
        out_shape=[
            jax.ShapeDtypeStruct((slots, BLK, BLK), jnp.float32),
            jax.ShapeDtypeStruct((2, db, rows, BLK), bf),
            jax.ShapeDtypeStruct((qw, BLK, 2 * rows), bf),
            jax.ShapeDtypeStruct((8, lanes), jnp.int32),
        ],
        in_specs=[vmem] + [hbm] * 2,
        out_specs=[hbm] * 4,
        scratch_shapes=[pltpu.VMEM((2, per_t, rows, BLK), bf)] + [pltpu.VMEM((2, db, rows, BLK), bf)] * 4
        + [pltpu.VMEM((2, rows, hw * BLK), bf)]
        + [pltpu.VMEM((2, rows, qw * BLK), bf)] * 2
        + [pltpu.VMEM((qw, BLK, 2 * rows), bf), pltpu.VMEM((slots, BLK, BLK), jnp.float32)]
        + [pltpu.VMEM((2, rows, dm), bf), pltpu.VMEM((2, rows, qw * BLK), bf), dma((3,)),
           pltpu.VMEM((8, lanes), jnp.int32), pltpu.SMEM((8, lanes), jnp.int32), dma((5,))]
        + [dma((4,)), dma((4,)), dma((nch + 2,)), dma((nch + 2,)), dma((2,)), dma((2,)), dma((nch,)), dma((nch,)),
           dma((4,)), dma((4,)), dma((n_tc,)), dma((n_tc,))],
        compiler_params=pltpu.CompilerParams(
            collective_id=0, has_side_effects=True, vmem_limit_bytes=40 * 1024 * 1024),
        cost_estimate=pl.CostEstimate(
            flops=slots * BLK * BLK * rows * 12, bytes_accessed=16 * 1024 * 1024, transcendentals=0),
    )(jnp.transpose(block_mask, (1, 0, 2)),
      hidden.reshape(2, rows, ff), incoming.reshape(2, rows, dm))
    per_step = pl.BlockSpec((unroll, BLK, BLK), lambda g: (g, 0, 0))
    out = pl.pallas_call(
        functools.partial(last_pass, unroll),
        grid=(slots // unroll,),
        out_shape=jax.ShapeDtypeStruct((slots, BLK, BLK), bf),
        in_specs=[pl.BlockSpec(memory_space=pltpu.SMEM), vmem, vmem, per_step],
        out_specs=per_step,
        compiler_params=pltpu.CompilerParams(vmem_limit_bytes=32 * 1024 * 1024),
        cost_estimate=pl.CostEstimate(
            flops=slots * BLK * BLK * rows * 4, bytes_accessed=16 * 1024 * 1024, transcendentals=0),
    )(tab, turned, cot, acc)
    return out.reshape(1, 1, slots, BLK, BLK)


def solution(mesh):
    placed = (
        P(None, "section", "mirror", None, "tp"),
        P(None, "section", "mirror", None, "tp"),
        P(None, "tp", None),
    )
    return jax.shard_map(
        body,
        mesh=mesh,
        in_specs=placed,
        out_specs=P("section", "tp", "mirror", None, None),
        check_vma=False,
    )
```
